256 devices in a mesh: seq: 128 (over y, z, x), chan: 2 (over core).
Axes of the slice: x: 4, y: 4, z: 8, core: 2. Of those that a mesh axis runs over, the one named last changes fastest.
Arguments:
- tower_input: bfloat16 [32768, 1536], P('seq', 'chan'), may hold values from -16 to 16, as said below
- dilated_weight: bfloat16 [3, 1536, 1536], P(None, None, 'chan'), may hold values from -0.09375 to 0.09375
- norm_gain: float32 [1536], replicated, may hold values from 0.5 to 1.5
- track_embed: bfloat16 [512, 1536], P('seq', 'chan'), may hold values from -16 to 16
- span_start: int32 [2048], replicated, may hold values from 0 to 32767, as said below
- span_end: int32 [2048], replicated, may hold values from 1 to 32768, as said below
- span_owner: int32 [2048], replicated, may hold values from 0 to 511, as said below
- positive: int32 [512], P('seq'), may hold values from 0 to 511, each once
Outputs:
- grad_input: float32 [32768, 1536], P('seq', 'chan')
- loss: float32 [], replicated
The draws below stay inside these ranges and needn't reach their ends.
Inputs may be any that keep to these rules, and one draw needn't show every extreme that they name: `tower_input`: values of the bins' embeddings. Span s covers the bins span_start[s] to span_end[s] - 1; span 0 covers bin 0 alone. span_end[s] > span_start[s]; the last span covers bin 32768 - 1 alone. `span_owner`: every gene owns at least one span; spans of one gene may lie anywhere and may share bins with spans of other genes.
All inputs are finite; a program needn't handle non-finite values.
Results may differ from the reference program's by a relative error of at most 0.01.
Values may be sent and summed in bfloat16 or wider, within the bound.
A program may use at most 64 MiB of HBM per device.

```python
import jax
import jax.numpy as jnp
from jax import lax

C = 1536
L_DEV = 256
DILATION_STEP = 128
WINDOW_BINS = 32768
GENES = 512
SPANS = 2048
N_SEQ = 128


def span_table(key):
    key = jax.random.fold_in(key, 101)
    keys = jax.random.split(key, 6)
    first = jax.random.randint(keys[0], (SPANS,), 0, WINDOW_BINS)
    second = jax.random.randint(keys[1], (SPANS,), 0, WINDOW_BINS)
    anchor = jnp.minimum(first, second)
    raw = jax.random.randint(keys[2], (SPANS,), 0, 4 * L_DEV)
    shifts = jax.random.randint(keys[3], (SPANS,), 0, 7)
    length = 1 + jnp.right_shift(raw, shifts)
    index = jnp.arange(SPANS, dtype=jnp.int32)
    length = jnp.where((index == 0) | (index == SPANS - 1), 1, length)
    start = jnp.minimum(anchor, WINDOW_BINS - length)
    start = jnp.where(index == 0, 0, start)
    start = jnp.where(index == SPANS - 1, WINDOW_BINS - length, start)
    end = start + length
    order = jax.random.permutation(keys[4], GENES).astype(jnp.int32)
    extra = jax.random.randint(keys[5], (SPANS,), 4, GENES)
    slot = jnp.where(index < GENES, index, extra)
    owner = order[slot]
    return (start.astype(jnp.int32), end.astype(jnp.int32), owner.astype(jnp.int32))


def draw_span_start(key, part):
    return span_table(key)[0]


def draw_span_end(key, part):
    return span_table(key)[1]


def draw_span_owner(key, part):
    return span_table(key)[2]


def draw_tower_input(key, part):
    key = jax.random.fold_in(key, 1)
    values = jnp.clip(jax.random.normal(key, (WINDOW_BINS, C), jnp.float32), -6.0, 6.0)
    return values.astype(jnp.bfloat16)


def draw_track_embed(key, part):
    key = jax.random.fold_in(key, 2)
    values = jnp.clip(3.0 * jax.random.normal(key, (GENES, C), jnp.float32), -15.0, 15.0)
    return values.astype(jnp.bfloat16)


def shard_levels(rng, shape, shards, least, top_value):
    level = 1.0
    for position, shards_of in shards:
        steps = jax.random.uniform(jax.random.fold_in(jax.random.fold_in(rng, 6), position), (shards_of,), jnp.float32, least / len(shards), top_value / len(shards))
        level = level * jnp.repeat(jnp.exp(steps), shape[position] // shards_of).reshape((-1,) + (1,) * (len(shape) - 1 - position))
    return level


def bell_draw(own_key, shape, scale, most, cuts=(), kind=jnp.bfloat16):
    factor_of = shard_levels(own_key, shape, cuts, -0.22, 0.18) if cuts else 1.0
    drawn = jax.random.normal(own_key, shape, jnp.float32) * scale * factor_of
    return jnp.minimum(jnp.maximum(drawn, -most), most).astype(kind)


def setup_inputs(seed: int = 0) -> dict:
    splits = jax.random.split(jax.random.key(seed), 9)
    tower_input = draw_tower_input(jax.random.fold_in(splits[8], 71), 0)
    dilated_weight = bell_draw(splits[1], (3, C, C), (3 * C) ** -0.5, 0.09375, ((2, 2),))
    norm_gain = jnp.clip(1.0 + 0.1 * jax.random.normal(splits[2], (C,), jnp.float32), 0.5, 1.5)
    track_embed = draw_track_embed(jax.random.fold_in(splits[8], 71), 0)
    span_start = draw_span_start(jax.random.fold_in(splits[8], 71), 0)
    span_end = draw_span_end(jax.random.fold_in(splits[8], 71), 0)
    span_owner = draw_span_owner(jax.random.fold_in(splits[8], 71), 0)
    positive = jax.random.permutation(splits[7], GENES).astype(jnp.int32)
    return dict(tower_input=tower_input, dilated_weight=dilated_weight, norm_gain=norm_gain, track_embed=track_embed, span_start=span_start, span_end=span_end, span_owner=span_owner, positive=positive)


epsilon = 1e-06
inverse_temp = 2.0
loss_scale = 64.0

def activate(values, gain):
    mean_sq = lax.optimization_barrier(jnp.mean(values * values, axis=-1, keepdims=True))
    normed = values * lax.rsqrt(mean_sq + epsilon) * gain
    return (normed, jax.nn.gelu(normed))

def norm_back(values, gain, activated_gradient):
    mean_sq = lax.optimization_barrier(jnp.mean(values * values, axis=-1, keepdims=True))
    inv_root = lax.rsqrt(mean_sq + epsilon)
    normed = values * inv_root * gain
    _, pull = jax.vjp(jax.nn.gelu, normed)
    scaled = gain * pull(activated_gradient)[0]
    inner = lax.optimization_barrier(jnp.mean(values * scaled, axis=-1, keepdims=True))
    return inv_root * scaled - values * inv_root * inv_root * inv_root * inner

def block_counts(index, span_start, span_end, owner_hot):
    positions = index * L_DEV + jnp.arange(L_DEV, dtype=jnp.int32)
    member = ((span_start[:, None] <= positions[None, :]) & (positions[None, :] < span_end[:, None])).astype(jnp.bfloat16)
    return jnp.dot(owner_hot, member, preferred_element_type=jnp.float32).astype(jnp.bfloat16)

def reference(tower_input, dilated_weight, norm_gain, track_embed, span_start, span_end, span_owner, positive):
    x = tower_input.astype(jnp.float32)
    _, activated_rows = activate(x, norm_gain)
    activated_rows = activated_rows.astype(jnp.bfloat16)
    bordered_input = jnp.pad(activated_rows, ((DILATION_STEP, DILATION_STEP), (0, 0)))
    convolved_output = jnp.dot(bordered_input[0:WINDOW_BINS], dilated_weight[0], preferred_element_type=jnp.float32)
    convolved_output = convolved_output + jnp.dot(bordered_input[DILATION_STEP:DILATION_STEP + WINDOW_BINS], dilated_weight[1], preferred_element_type=jnp.float32)
    convolved_output = convolved_output + jnp.dot(bordered_input[2 * DILATION_STEP:2 * DILATION_STEP + WINDOW_BINS], dilated_weight[2], preferred_element_type=jnp.float32)
    hidden = (x + convolved_output).astype(jnp.bfloat16)
    owner_hot = (span_owner[None, :] == jnp.arange(GENES, dtype=jnp.int32)[:, None]).astype(jnp.bfloat16)

    def pool_step(total, index):
        counts = block_counts(index, span_start, span_end, owner_hot)
        sequence_rows = lax.dynamic_slice_in_dim(hidden, index * L_DEV, L_DEV, 0)
        return (total + jnp.dot(counts, sequence_rows, preferred_element_type=jnp.float32), None)
    pooled, _ = lax.scan(pool_step, jnp.zeros((GENES, C), jnp.float32), jnp.arange(N_SEQ, dtype=jnp.int32))
    width = float(C)
    scale = lax.rsqrt(lax.optimization_barrier(jnp.mean(pooled * pooled, axis=1)) + epsilon)
    unit = 1.0 / jnp.sqrt(jnp.float32(width))
    query = (pooled * scale[:, None] * unit).astype(jnp.bfloat16)
    logits = inverse_temp * jnp.dot(query, track_embed.T, preferred_element_type=jnp.float32)
    top = lax.optimization_barrier(jnp.max(logits, axis=1))
    log_total = top + jnp.log(lax.optimization_barrier(jnp.sum(jnp.exp(logits - top[:, None]), axis=1)))
    hits = jnp.arange(GENES, dtype=jnp.int32)[None, :] == positive[:, None]
    per_gene = log_total - lax.optimization_barrier(jnp.sum(jnp.where(hits, logits, 0.0), axis=1))
    loss = jnp.mean(per_gene)
    weights = jnp.exp(logits - log_total[:, None])
    grad_logit = (loss_scale * (weights - hits.astype(jnp.float32))).astype(jnp.bfloat16)
    grad_query = inverse_temp * jnp.dot(grad_logit, track_embed, preferred_element_type=jnp.float32)
    inner = lax.optimization_barrier(jnp.sum(grad_query * pooled, axis=1))
    grad_pooled = (unit * scale[:, None] * (grad_query - pooled * (inner * scale * scale / width)[:, None])).astype(jnp.bfloat16)

    def unpool_block(index):
        counts = block_counts(index, span_start, span_end, owner_hot)
        return jnp.dot(counts.T, grad_pooled, preferred_element_type=jnp.float32).astype(jnp.bfloat16)
    hidden_gradient = lax.map(unpool_block, jnp.arange(N_SEQ, dtype=jnp.int32)).reshape(WINDOW_BINS, C)
    border_gradient = jnp.pad(hidden_gradient, ((DILATION_STEP, DILATION_STEP), (0, 0)))
    activated_gradient = jnp.dot(border_gradient[2 * DILATION_STEP:2 * DILATION_STEP + WINDOW_BINS], dilated_weight[0].T, preferred_element_type=jnp.float32)
    activated_gradient = activated_gradient + jnp.dot(border_gradient[DILATION_STEP:DILATION_STEP + WINDOW_BINS], dilated_weight[1].T, preferred_element_type=jnp.float32)
    activated_gradient = activated_gradient + jnp.dot(border_gradient[0:WINDOW_BINS], dilated_weight[2].T, preferred_element_type=jnp.float32)
    grad_input = hidden_gradient.astype(jnp.float32) + norm_back(x, norm_gain, activated_gradient)
    return (grad_input, loss)
```

```python
import functools

import jax
import jax.numpy as jnp
from jax import lax
from jax.experimental import pallas as pl
from jax.experimental.pallas import tpu as pltpu
from jax.sharding import PartitionSpec as P

STEP = 128
TAPS = 3
EPS = 1e-06
INV_TEMP = 2.0
LOSS_SCALE = 64.0
MESH = pl.DeviceIdType.MESH
F32 = jnp.float32
BF16 = jnp.bfloat16
ROWS = 32
PIECES = 2
GELU_A = 0.7978845608028654
GELU_B = 0.044715


def first_order(value, dims, genes_each):
    ny, nz, nx = dims
    place = lax.rem(value, genes_each)
    owner = lax.div(value, genes_each)
    x = lax.rem(owner, nx)
    z = lax.rem(lax.div(owner, nx), nz)
    y = lax.div(owner, nx * nz)
    return ((y * nx + x) * nz + z) * genes_each + place


def second_from_first(row, dims, genes_each):
    ny, nz, nx = dims
    place = lax.rem(row, genes_each)
    z = lax.rem(lax.div(row, genes_each), nz)
    plane = lax.div(row, genes_each * nz)
    return (z * (ny * nx) + plane) * genes_each + place


def dot_nt(a, b):
    return lax.dot_general(a, b, (((1,), (1,)), ((), ())), preferred_element_type=F32)


def dot_nn(a, b):
    return jnp.dot(a, b, preferred_element_type=F32)


def phases(dims):
    ny, nz, nx = dims
    planes = ny * nx
    sizes = (
        ("core", 1),
        ("next", PIECES),
        ("prev", PIECES),
        ("left", PIECES),
        ("right", PIECES),
        ("mid", 1),
        ("last", 2),
        ("track_a1", nz),
        ("track_a2", planes),
        ("track_b1", planes),
        ("track_b2", nz),
        ("pool_b1", nz),
        ("pool_a1", 2 * planes),
        ("pool_a2", nz),
        ("pool_b2", planes),
        ("grad_a1", nz),
        ("grad_a2", planes),
        ("grad_b1", planes),
        ("grad_b2", nz),
        ("loss", planes),
    )
    at, total = {}, 0
    for name, size in sizes:
        at[name] = total
        total += size
    return at, total


def kernel(
    dims,
    stop,
    x_hbm,
    w_hbm,
    gain_hbm,
    track_hbm,
    start_hbm,
    end_hbm,
    owner_hbm,
    positive_hbm,
    out_v,
    loss_ref,
    gain,
    track,
    start,
    end,
    owner,
    positive,
    xp,
    w,
    act,
    fac,
    xq,
    own_hot,
    member,
    counts,
    counts_t,
    counts_b,
    counts_tb,
    perm,
    perm_t,
    acc,
    hid,
    send_a,
    recv_a,
    send_b,
    recv_b,
    tmp_a,
    tmp_b,
    send_a2,
    recv_a2,
    send_b2,
    recv_b2,
    track_a1,
    track_b1,
    trk_a,
    trk_raw,
    trk_b,
    mid_out,
    mid_in,
    grad_a1,
    grad_b1,
    grad_a,
    grad_b,
    loss_out,
    loss_in,
    hg,
    ga_mine,
    ga_send,
    ga_recv,
    load_sem,
    send_sem,
    recv_sem,
):
    ny, nz, nx = dims
    nseq = ny * nz * nx
    planes = ny * nx
    rows, half = out_v.shape
    padded = rows + 2 * STEP
    width = 2 * half
    gl = track.shape[0]
    genes = gl * nseq
    group_a = gl * nz
    group_b = gl * planes
    cols = half // 3
    wide_a = 2 * cols
    first_sem, _ = phases(dims)
    me = lax.axis_index("seq")
    c = lax.axis_index("chan")
    oc = 1 - c
    x = lax.rem(me, nx)
    z = lax.rem(lax.div(me, nx), nz)
    y = lax.div(me, nx * nz)
    p = y * nx + x
    nxt = lax.rem(me + 1, nseq)
    prv = lax.rem(me + nseq - 1, nseq)

    def plane_at(q):
        return (lax.div(q, nx) * nz + z) * nx + lax.rem(q, nx)

    def plane_to(k):
        return lax.rem(p + k, planes)

    def plane_from(k):
        return lax.rem(p + planes - k, planes)

    def z_at(q):
        return (y * nz + q) * nx + x

    def z_to(k):
        return lax.rem(z + k, nz)

    def z_from(k):
        return lax.rem(z + nz - k, nz)

    def rows_a(q):
        return pl.ds(pl.multiple_of(q * group_a, group_a), group_a)

    def rows_b(q):
        return pl.ds(pl.multiple_of(q * group_b, group_b), group_b)

    def loop(lo, hi, body):
        def step(i, carry):
            body(i)
            return carry

        lax.fori_loop(lo, hi, step, 0)

    def remote(src, dst, name, k, seq, chan):
        return pltpu.make_async_remote_copy(
            src_ref=src,
            dst_ref=dst,
            send_sem=send_sem.at[first_sem[name] + k],
            recv_sem=recv_sem.at[first_sem[name] + k],
            device_id=(seq, chan),
            device_id_type=MESH,
        )

    barrier = pltpu.get_barrier_semaphore()

    def greet(seq, chan):
        pl.semaphore_signal(barrier, inc=1, device_id=(seq, chan), device_id_type=MESH)

    loop(1, nz, lambda k: greet(z_at(z_to(k)), c))
    loop(1, planes, lambda k: greet(plane_at(plane_to(k)), c))
    greet(nxt, c)
    greet(prv, c)
    greet(me, oc)

    mid_rows = pl.ds(STEP, rows)
    smalls = [
        pltpu.make_async_copy(src, dst, load_sem.at[4 + i])
        for i, (src, dst) in enumerate(
            (
                (track_hbm, track),
                (start_hbm, start),
                (end_hbm, end),
                (owner_hbm, owner),
                (gain_hbm, gain),
                (positive_hbm, positive),
            )
        )
    ]
    load_x = pltpu.make_async_copy(x_hbm, xp.at[c, mid_rows], load_sem.at[0])
    load_w = [
        pltpu.make_async_copy(w_hbm.at[k], w.at[k], load_sem.at[1 + k]) for k in range(TAPS)
    ]
    for copy in smalls:
        copy.start()
    load_x.start()
    for copy in smalls:
        copy.wait()
    own_track = track[...].astype(F32)
    track_a1[z] = own_track[:, 0:wide_a]
    track_b1[p] = own_track[:, wide_a:half]
    load_x.wait()
    pl.semaphore_wait(barrier, 3 + planes - 1 + nz - 1)

    piece = STEP // PIECES

    def to_next(i):
        src = pl.ds(rows + i * piece, piece)
        return remote(xp.at[c, src], xp.at[c, pl.ds(i * piece, piece)], "next", i, nxt, c)

    def to_prev(i):
        src = pl.ds(STEP + i * piece, piece)
        dst = pl.ds(STEP + rows + i * piece, piece)
        return remote(xp.at[c, src], xp.at[c, dst], "prev", i, prv, c)

    def core(side):
        return remote(xp.at[side, mid_rows], xp.at[side, mid_rows], "core", 0, me, oc)

    def left(side, i):
        some = pl.ds(i * piece, piece)
        return remote(xp.at[side, some], xp.at[side, some], "left", i, me, oc)

    def right(side, i):
        some = pl.ds(STEP + rows + i * piece, piece)
        return remote(xp.at[side, some], xp.at[side, some], "right", i, me, oc)

    for i in range(PIECES):
        to_next(i).start()
        to_prev(i).start()
    core(c).start()

    def gather_a1(buf, name, k, slot):
        return remote(buf.at[z], buf.at[slot], name, k, z_at(z_to(k)), c)

    def gather_b1(buf, name, k, slot):
        return remote(buf.at[p], buf.at[slot], name, k, plane_at(plane_to(k)), c)

    def gather_a2(buf, name, k, q):
        return remote(buf.at[rows_a(p)], buf.at[rows_a(q)], name, k, plane_at(plane_to(k)), c)

    def gather_b2(buf, name, k, q):
        return remote(buf.at[rows_b(z)], buf.at[rows_b(q)], name, k, z_at(z_to(k)), c)

    loop(1, nz, lambda k: gather_a1(track_a1, "track_a1", k, z).start())
    loop(1, planes, lambda k: gather_b1(track_b1, "track_b1", k, p).start())
    for copy in load_w:
        copy.start()

    first = start[...]
    last = end[...]
    slot_of = first_order(owner[...], dims, gl)
    spans = first.shape[1]
    base = me * rows - STEP

    def member_rows(i):
        at = pl.multiple_of(i * ROWS, ROWS)
        bins = base + at + lax.broadcasted_iota(jnp.int32, (ROWS, spans), 0)
        inside = (first <= bins) & (bins < last)
        member[pl.ds(at, ROWS), :] = jnp.where(inside, 1.0, 0.0).astype(BF16)

    def owner_rows(i):
        at = pl.multiple_of(i * ROWS, ROWS)
        gene = at + lax.broadcasted_iota(jnp.int32, (ROWS, spans), 0)
        own_hot[pl.ds(at, ROWS), :] = jnp.where(slot_of == gene, 1.0, 0.0).astype(BF16)

    def perm_rows(i):
        at = pl.multiple_of(i * ROWS, ROWS)
        down = at + lax.broadcasted_iota(jnp.int32, (ROWS, genes), 0)
        across = lax.broadcasted_iota(jnp.int32, (1, genes), 1)
        moved = second_from_first(at + lax.broadcasted_iota(jnp.int32, (ROWS, 1), 0), dims, gl)
        some = pl.ds(at, ROWS)
        perm[some, :] = jnp.where(across == moved, 1.0, 0.0).astype(BF16)
        across = second_from_first(across, dims, gl)
        perm_t[some, :] = jnp.where(across == down, 1.0, 0.0).astype(BF16)

    loop(0, genes // ROWS, owner_rows)
    loop(0, padded // ROWS, member_rows)

    def normed_rows(at):
        some = pl.ds(at, ROWS)
        x0 = xp[0, some, :].astype(F32)
        x1 = xp[1, some, :].astype(F32)
        total = jnp.sum(x0 * x0, axis=1, keepdims=True) + jnp.sum(x1 * x1, axis=1, keepdims=True)
        root = lax.rsqrt(total / width + EPS)
        return (x0, x1), root

    def gain_of(h):
        return gain[h * half : (h + 1) * half].reshape(1, half)

    def gelu(n):
        return 0.5 * n * (1.0 + jnp.tanh(GELU_A * (n + GELU_B * n * n * n)))

    def gelu_slope(n):
        t = jnp.tanh(GELU_A * (n + GELU_B * n * n * n))
        return 0.5 * (1.0 + t) + 0.5 * n * (1.0 - t * t) * (
            GELU_A * (1.0 + 3.0 * GELU_B * n * n)
        )

    def activate(lo, count, keep):
        def body(i):
            at = pl.multiple_of(lo + i * ROWS, ROWS)
            xs, root = normed_rows(at)
            for h in range(2):
                act[h, pl.ds(at, ROWS), :] = (gelu(xs[h] * root * gain_of(h)) * keep).astype(BF16)

        loop(0, count // ROWS, body)

    core(oc).wait_recv()
    activate(STEP, rows, 1.0)

    for copy in load_w:
        copy.wait()

    def tap(lo, count, k, some):
        return dot_nn(act[0, lo : lo + count, :], w[k, 0:half, some]) + dot_nn(
            act[1, lo : lo + count, :], w[k, half:width, some]
        )

    def centre_cols(i):
        some = pl.ds(pl.multiple_of(i * cols, cols), cols)
        acc[:, some] = xp[c, mid_rows, some].astype(F32) + tap(STEP, rows, 1, some)
        acc[0:STEP, some] += tap(rows, STEP, 2, some)
        acc[STEP:rows, some] += tap(STEP, STEP, 0, some)

    loop(0, half // cols, centre_cols)

    def gather_turn(a1, b1, a2, b2, name):
        def a_wait(k):
            gather_a1(a1, name + "_a1", k, z_from(k)).wait_recv()

        loop(1, nz, a_wait)
        for i in range(nz):
            tmp_a[i * gl : (i + 1) * gl, :] = a1[i, :, 0:wide_a]
        a2[rows_a(p), :] = tmp_a[...].astype(BF16)
        loop(1, planes, lambda k: gather_a2(a2, name + "_a2", k, p).start())

        def b_wait(k):
            gather_b1(b1, name + "_b1", k, plane_from(k)).wait_recv()

        loop(1, planes, b_wait)
        for i in range(planes):
            tmp_b[i * gl : (i + 1) * gl, :] = b1[i]
        b2[rows_b(z), :] = tmp_b[...].astype(BF16)
        loop(1, nz, lambda k: gather_b2(b2, name + "_b2", k, z).start())

    def gather_end_a(a2, name):
        def a_wait(k):
            gather_a2(a2, name + "_a2", k, plane_from(k)).wait_recv()

        loop(1, planes, a_wait)

    def gather_end_b(b2, name):
        def b_wait(k):
            gather_b2(b2, name + "_b2", k, z_from(k)).wait_recv()

        loop(1, nz, b_wait)

    gather_turn(track_a1, track_b1, trk_a, trk_raw, "track")

    tile = min(256, genes)

    def count_rows(i):
        some = pl.ds(pl.multiple_of(i * tile, tile), tile)
        counts[some, :] = dot_nt(own_hot[some, :], member[mid_rows, :]).astype(BF16)

    keep_left = jnp.where(me > 0, 1.0, 0.0)
    keep_right = jnp.where(me < nseq - 1, 1.0, 0.0)
    for i in range(PIECES):
        to_next(i).wait_recv()
        left(c, i).start()
        to_prev(i).wait_recv()
        right(c, i).start()
        if i == 0:
            loop(0, genes // tile, count_rows)
            loop(0, genes // ROWS, perm_rows)
        else:
            counts_b[...] = dot_nn(perm_t[...], counts[...]).astype(BF16)
        left(oc, i).wait_recv()
        activate(i * piece, piece, keep_left)
        right(oc, i).wait_recv()
        activate(STEP + rows + i * piece, piece, keep_right)

    def hidden_cols(i):
        some = slice(i * cols, (i + 1) * cols)
        hid[0:STEP, some] = (acc[0:STEP, some] + tap(0, STEP, 0, some)).astype(BF16)
        hid[STEP:rows, some] = (acc[STEP:rows, some] + tap(STEP + rows, STEP, 2, some)).astype(BF16)
        return hid[:, some]

    def pool_b1(k):
        q = z_to(k)
        return remote(send_b.at[rows_b(q)], recv_b.at[k], "pool_b1", k, z_at(q), c)

    def pool_a1(i, k):
        q = plane_to(k)
        return remote(
            send_a.at[i, rows_a(q)],
            recv_a.at[i, k],
            "pool_a1",
            i * planes + k,
            plane_at(q),
            c,
        )

    send_b[...] = dot_nn(counts_b[...], hidden_cols(2)).astype(BF16)
    loop(1, nz, lambda k: pool_b1(k).start())
    for i in range(2):
        send_a[i] = dot_nn(counts[...], hidden_cols(i)).astype(BF16)
        loop(1, planes, lambda k: pool_a1(i, k).start())

    def factor_rows(i):
        at = pl.multiple_of(i * ROWS, ROWS)
        some = pl.ds(at, ROWS)
        xs, root = normed_rows(STEP + at)
        for h in range(2):
            g = gain_of(h)
            fac[h, some, :] = gelu_slope(xs[h] * root * g) * (root * g)
        xq[some, :] = jnp.where(c == 0, xs[0], xs[1]) * (root * root / width)

    loop(0, rows // ROWS, factor_rows)

    def pool_b2(k):
        q = plane_to(k)
        return remote(send_b2.at[q], recv_b2.at[k], "pool_b2", k, plane_at(q), c)

    def pool_a2(k):
        q = z_to(k)
        return remote(send_a2.at[q], recv_a2.at[k], "pool_a2", k, z_at(q), c)

    def sum_b1(k, total):
        pool_b1(k).wait_recv()
        return total + recv_b[k].astype(F32)

    tmp_b[...] = lax.fori_loop(1, nz, sum_b1, send_b[rows_b(z), :].astype(F32))
    for i in range(planes):
        send_b2[i] = tmp_b[i * gl : (i + 1) * gl, :]
    loop(1, planes, lambda k: pool_b2(k).start())

    for i in range(2):

        def sum_a1(k, total):
            pool_a1(i, k).wait_recv()
            return total + recv_a[i, k].astype(F32)

        tmp_a[:, i * cols : (i + 1) * cols] = lax.fori_loop(
            1, planes, sum_a1, send_a[i, rows_a(p), :].astype(F32)
        )
    for i in range(nz):
        send_a2[i] = tmp_a[i * gl : (i + 1) * gl, :]
    loop(1, nz, lambda k: pool_a2(k).start())

    def count_cols(i):
        some = pl.ds(pl.multiple_of(i * STEP, STEP), STEP)
        counts_t[some, :] = dot_nt(member[some, :], own_hot[...]).astype(BF16)
        counts_tb[some, :] = dot_nn(counts_t[some, :], perm[...]).astype(BF16)

    loop(0, padded // STEP, count_cols)
    gather_end_a(trk_a, "track")
    gather_end_b(trk_raw, "track")
    trk_b[...] = dot_nn(perm[...], trk_raw[...]).astype(BF16)

    def sum_b2(k, total):
        pool_b2(k).wait_recv()
        return total + recv_b2[k]

    mine_b = lax.fori_loop(1, planes, sum_b2, send_b2[p])

    def sum_a2(k, total):
        pool_a2(k).wait_recv()
        return total + recv_a2[k]

    mine_a = lax.fori_loop(1, nz, sum_a2, send_a2[z])

    raw_part = dot_nt(mine_a.astype(BF16), trk_a[...]) + dot_nt(mine_b.astype(BF16), trk_b[...])
    sq_part = jnp.sum(mine_a * mine_a, axis=1, keepdims=True) + jnp.sum(
        mine_b * mine_b, axis=1, keepdims=True
    )
    mid_out[:, 0:genes] = raw_part
    mid_out[:, genes : genes + 128] = jnp.broadcast_to(sq_part, (gl, 128))
    mid = remote(mid_out, mid_in, "mid", 0, me, oc)
    mid.start()
    mid.wait_recv()
    both = mid_out[...] + mid_in[...]
    raw = both[:, 0:genes]
    scale = lax.rsqrt(both[:, genes : genes + 1] / width + EPS)
    unit = float(width) ** -0.5
    logits = raw * (scale * (INV_TEMP * unit))
    top = jnp.max(logits, axis=1, keepdims=True)
    log_total = top + jnp.log(jnp.sum(jnp.exp(logits - top), axis=1, keepdims=True))
    place = lax.broadcasted_iota(jnp.int32, (gl, genes), 0)
    want = jnp.zeros((gl, genes), jnp.int32)
    for i in range(gl):
        want = jnp.where(place == i, first_order(positive[i], dims, gl), want)
    hits = lax.broadcasted_iota(jnp.int32, (gl, genes), 1) == want
    weights = jnp.exp(logits - log_total)
    grad_logit = (LOSS_SCALE * (weights - jnp.where(hits, 1.0, 0.0))).astype(BF16)
    inner = INV_TEMP * jnp.sum(grad_logit.astype(F32) * raw, axis=1, keepdims=True)
    back = inner * scale * scale / width
    outer = unit * scale
    grad_b1[p] = outer * (INV_TEMP * dot_nn(grad_logit, trk_b[...]) - mine_b * back)
    loop(1, planes, lambda k: gather_b1(grad_b1, "grad_b1", k, p).start())
    per_gene = log_total - jnp.sum(jnp.where(hits, logits, 0.0), axis=1, keepdims=True)
    grad_a1[z, :, 0:wide_a] = outer * (INV_TEMP * dot_nn(grad_logit, trk_a[...]) - mine_a * back)
    grad_a1[z, :, wide_a : wide_a + 128] = jnp.broadcast_to(per_gene, (gl, 128))
    loop(1, nz, lambda k: gather_a1(grad_a1, "grad_a1", k, z).start())

    gather_turn(grad_a1, grad_b1, grad_a, grad_b, "grad")
    part = jnp.zeros((1, 128), F32)
    for i in range(nz):
        part = part + jnp.sum(grad_a1[i, :, wide_a : wide_a + 128], axis=0, keepdims=True)
    loss_out[...] = jnp.broadcast_to(part, (8, 128))
    loss_in[p] = loss_out[...]

    def loss_copy(k, q):
        return remote(loss_out, loss_in.at[q], "loss", k, plane_at(plane_to(k)), c)

    loop(1, planes, lambda k: loss_copy(k, p).start())

    gather_end_b(grad_b, "grad")

    def hidden_grad_b(i):
        some = pl.ds(pl.multiple_of(i * STEP, STEP), STEP)
        hg[some, wide_a:half] = dot_nn(counts_tb[some, :], grad_b[...]).astype(BF16)

    loop(0, padded // STEP, hidden_grad_b)
    gather_end_a(grad_a, "grad")

    def hidden_grad_a(i):
        some = pl.ds(pl.multiple_of(i * STEP, STEP), STEP)
        hg[some, 0:wide_a] = dot_nn(counts_t[some, :], grad_a[...]).astype(BF16)

    loop(0, padded // STEP, hidden_grad_a)

    def activ_grad(h):
        def body(i):
            at = pl.multiple_of(i * cols, cols)
            wide = pl.ds(pl.multiple_of(h * half + at, cols), cols)
            total = jnp.zeros((rows, cols), F32)
            for k in range(TAPS):
                lo = (TAPS - 1 - k) * STEP
                total = total + dot_nt(hg[lo : lo + rows, :], w[k, wide, :])
            ga_mine[h, :, pl.ds(at, cols)] = total
            ga_send[h, :, pl.ds(at, cols)] = total.astype(BF16)

        loop(0, half // cols, body)

    def grad_copy(h, i):
        return remote(ga_send.at[h], ga_recv.at[h], "last", i, me, oc)

    activ_grad(oc)
    grad_copy(oc, 0).start()
    activ_grad(c)
    grad_copy(c, 1).start()

    def loss_wait(k):
        loss_copy(k, plane_from(k)).wait_recv()

    loop(1, planes, loss_wait)
    total_loss = jnp.zeros((8, 128), F32)
    for i in range(planes):
        total_loss = total_loss + loss_in[i]
    loss_ref[...] = total_loss[0:1, 0:1] / genes

    for i in range(PIECES):
        to_next(i).wait_send()
        to_prev(i).wait_send()
        left(c, i).wait_send()
        right(c, i).wait_send()
    core(c).wait_send()
    mid.wait_send()

    def z_sent(k):
        gather_a1(track_a1, "track_a1", k, z).wait_send()
        gather_b2(trk_raw, "track_b2", k, z).wait_send()
        pool_b1(k).wait_send()
        pool_a2(k).wait_send()
        gather_a1(grad_a1, "grad_a1", k, z).wait_send()
        gather_b2(grad_b, "grad_b2", k, z).wait_send()

    loop(1, nz, z_sent)

    def plane_sent(k):
        gather_b1(track_b1, "track_b1", k, p).wait_send()
        gather_a2(trk_a, "track_a2", k, p).wait_send()
        pool_a1(0, k).wait_send()
        pool_a1(1, k).wait_send()
        pool_b2(k).wait_send()
        gather_b1(grad_b1, "grad_b1", k, p).wait_send()
        gather_a2(grad_a, "grad_a2", k, p).wait_send()
        loss_copy(k, p).wait_send()

    loop(1, planes, plane_sent)
    grad_copy(c, 0).wait_recv()
    grad_copy(oc, 1).wait_recv()

    def finish(i):
        at = pl.multiple_of(i * ROWS, ROWS)
        some = pl.ds(at, ROWS)
        wide = pl.ds(STEP + at, ROWS)
        v = []
        total = jnp.zeros((ROWS, 1), F32)
        for h in range(2):
            v.append(fac[h, some, :] * (ga_mine[h, some, :] + ga_recv[h, some, :].astype(F32)))
            total = total + jnp.sum(xp[h, wide, :].astype(F32) * v[h], axis=1, keepdims=True)
        own = jnp.where(c == 0, v[0], v[1])
        out_v[some, :] = hg[wide, :].astype(F32) + own - xq[some, :] * total

    loop(0, rows // ROWS, finish)
    grad_copy(oc, 0).wait_send()
    grad_copy(c, 1).wait_send()


def per_device(dims, stop, x, weight, gain, track, start, end, owner, positive):
    ny, nz, nx = dims
    nseq, planes = ny * nz * nx, ny * nx
    rows, half = x.shape
    gl = track.shape[0]
    genes, spans = gl * nseq, start.shape[0]
    group_a, group_b = gl * nz, gl * planes
    padded = rows + 2 * STEP
    cols = half // 3
    wide_a = 2 * cols
    copies = phases(dims)[1]
    dma = pltpu.SemaphoreType.DMA
    vmem = pl.BlockSpec(memory_space=pltpu.VMEM)
    scratch = [
        pltpu.VMEM((2 * half,), F32),
        pltpu.VMEM((gl, half), BF16),
        pltpu.VMEM((1, spans), jnp.int32),
        pltpu.VMEM((1, spans), jnp.int32),
        pltpu.VMEM((1, spans), jnp.int32),
        pltpu.SMEM((gl,), jnp.int32),
        pltpu.VMEM((2, padded, half), BF16),
        pltpu.VMEM((TAPS, 2 * half, half), BF16),
        pltpu.VMEM((2, padded, half), BF16),
        pltpu.VMEM((2, rows, half), F32),
        pltpu.VMEM((rows, half), F32),
        pltpu.VMEM((genes, spans), BF16),
        pltpu.VMEM((padded, spans), BF16),
        pltpu.VMEM((genes, rows), BF16),
        pltpu.VMEM((padded, genes), BF16),
        pltpu.VMEM((genes, rows), BF16),
        pltpu.VMEM((padded, genes), BF16),
        pltpu.VMEM((genes, genes), BF16),
        pltpu.VMEM((genes, genes), BF16),
        pltpu.VMEM((rows, half), F32),
        pltpu.VMEM((rows, half), BF16),
        pltpu.VMEM((2, genes, cols), BF16),
        pltpu.VMEM((2, planes, group_a, cols), BF16),
        pltpu.VMEM((genes, cols), BF16),
        pltpu.VMEM((nz, group_b, cols), BF16),
        pltpu.VMEM((group_a, wide_a), F32),
        pltpu.VMEM((group_b, cols), F32),
        pltpu.VMEM((nz, gl, wide_a), F32),
        pltpu.VMEM((nz, gl, wide_a), F32),
        pltpu.VMEM((planes, gl, cols), F32),
        pltpu.VMEM((planes, gl, cols), F32),
        pltpu.VMEM((nz, gl, wide_a), F32),
        pltpu.VMEM((planes, gl, cols), F32),
        pltpu.VMEM((genes, wide_a), BF16),
        pltpu.VMEM((genes, cols), BF16),
        pltpu.VMEM((genes, cols), BF16),
        pltpu.VMEM((gl, genes + 128), F32),
        pltpu.VMEM((gl, genes + 128), F32),
        pltpu.VMEM((nz, gl, wide_a + 128), F32),
        pltpu.VMEM((planes, gl, cols), F32),
        pltpu.VMEM((genes, wide_a), BF16),
        pltpu.VMEM((genes, cols), BF16),
        pltpu.VMEM((8, 128), F32),
        pltpu.VMEM((planes, 8, 128), F32),
        pltpu.VMEM((padded, half), BF16),
        pltpu.VMEM((2, rows, half), F32),
        pltpu.VMEM((2, rows, half), BF16),
        pltpu.VMEM((2, rows, half), BF16),
        dma((10,)),
        dma((copies,)),
        dma((copies,)),
    ]
    grad, loss = pl.pallas_call(
        functools.partial(kernel, dims, stop),
        out_shape=(
            jax.ShapeDtypeStruct((rows, half), F32),
            jax.ShapeDtypeStruct((1, 1), F32),
        ),
        in_specs=[pl.BlockSpec(memory_space=pltpu.HBM)] * 8,
        out_specs=(vmem, vmem),
        scratch_shapes=scratch,
        compiler_params=pltpu.CompilerParams(
            collective_id=0, has_side_effects=True, vmem_limit_bytes=48 * 1024 * 1024
        ),
    )(
        *(
            pltpu.with_memory_space_constraint(array, pltpu.HBM)
            for array in (
                x,
                weight,
                gain,
                track,
                start.reshape(1, -1),
                end.reshape(1, -1),
                owner.reshape(1, -1),
                positive,
            )
        )
    )
    return grad, loss.reshape(())


def solution(mesh, dims=(4, 8, 4), stop=99):
    return jax.shard_map(
        functools.partial(per_device, dims, stop),
        mesh=mesh,
        in_specs=(
            P("seq", "chan"),
            P(None, None, "chan"),
            P(),
            P("seq", "chan"),
            P(),
            P(),
            P(),
            P("seq"),
        ),
        out_specs=(P("seq", "chan"), P()),
        check_vma=False,
    )
```

```python
import functools

import jax
import jax.numpy as jnp
from jax import lax
from jax.experimental import pallas as pl
from jax.experimental.pallas import tpu as pltpu
from jax.sharding import PartitionSpec as P

STEP = 128
TAPS = 3
EPS = 1e-06
INV_TEMP = 2.0
LOSS_SCALE = 64.0
MESH = pl.DeviceIdType.MESH
F32 = jnp.float32
BF16 = jnp.bfloat16
ROWS = 32
PIECES = 2
GELU_A = 0.7978845608028654
GELU_B = 0.044715


def first_order(value, dims, genes_each):
    ny, nz, nx = dims
    place = lax.rem(value, genes_each)
    owner = lax.div(value, genes_each)
    x = lax.rem(owner, nx)
    z = lax.rem(lax.div(owner, nx), nz)
    y = lax.div(owner, nx * nz)
    return ((y * nx + x) * nz + z) * genes_each + place


def second_from_first(row, dims, genes_each):
    ny, nz, nx = dims
    place = lax.rem(row, genes_each)
    z = lax.rem(lax.div(row, genes_each), nz)
    plane = lax.div(row, genes_each * nz)
    return (z * (ny * nx) + plane) * genes_each + place


def dot_nt(a, b):
    return lax.dot_general(a, b, (((1,), (1,)), ((), ())), preferred_element_type=F32)


def dot_nn(a, b):
    return jnp.dot(a, b, preferred_element_type=F32)


def phases(dims):
    ny, nz, nx = dims
    planes = ny * nx
    sizes = (
        ("core", 1),
        ("next", PIECES),
        ("prev", PIECES),
        ("left", PIECES),
        ("right", PIECES),
        ("mid", 1),
        ("last", 3),
        ("dots", PIECES),
        ("track_a1", nz),
        ("track_a2", planes),
        ("track_b1", planes),
        ("track_b2", nz),
        ("pool_b1", nz),
        ("pool_a1", 2 * planes),
        ("pool_a2", nz),
        ("pool_b2", planes),
        ("grad_a1", nz),
        ("grad_a2", planes),
        ("grad_b1", planes),
        ("grad_b2", nz),
        ("loss", planes),
    )
    at, total = {}, 0
    for name, size in sizes:
        at[name] = total
        total += size
    return at, total


def kernel(
    dims,
    stop,
    x_hbm,
    w_hbm,
    gain_hbm,
    track_hbm,
    start_hbm,
    end_hbm,
    owner_hbm,
    positive_hbm,
    out_v,
    loss_ref,
    gain,
    track,
    start,
    end,
    owner,
    positive,
    xp,
    w,
    act,
    fac,
    xq,
    own_hot,
    member,
    counts,
    counts_t,
    counts_b,
    counts_tb,
    perm,
    perm_t,
    acc,
    hid,
    send_a,
    recv_a,
    send_b,
    recv_b,
    tmp_a,
    tmp_b,
    send_a2,
    recv_a2,
    send_b2,
    recv_b2,
    track_a1,
    track_b1,
    trk_a,
    trk_raw,
    trk_b,
    mid_out,
    mid_in,
    grad_a1,
    grad_b1,
    grad_a,
    grad_b,
    loss_out,
    loss_in,
    hg,
    ga_mine,
    ga_send,
    ga_recv,
    dots,
    dots_in,
    load_sem,
    send_sem,
    recv_sem,
):
    ny, nz, nx = dims
    nseq = ny * nz * nx
    planes = ny * nx
    rows, half = out_v.shape
    padded = rows + 2 * STEP
    width = 2 * half
    gl = track.shape[0]
    genes = gl * nseq
    group_a = gl * nz
    group_b = gl * planes
    cols = half // 3
    wide_a = 2 * cols
    first_sem, _ = phases(dims)
    me = lax.axis_index("seq")
    c = lax.axis_index("chan")
    oc = 1 - c
    x = lax.rem(me, nx)
    z = lax.rem(lax.div(me, nx), nz)
    y = lax.div(me, nx * nz)
    p = y * nx + x
    nxt = lax.rem(me + 1, nseq)
    prv = lax.rem(me + nseq - 1, nseq)

    def plane_at(q):
        return (lax.div(q, nx) * nz + z) * nx + lax.rem(q, nx)

    def plane_to(k):
        return lax.rem(p + k, planes)

    def plane_from(k):
        return lax.rem(p + planes - k, planes)

    def z_at(q):
        return (y * nz + q) * nx + x

    def z_to(k):
        return lax.rem(z + k, nz)

    def z_from(k):
        return lax.rem(z + nz - k, nz)

    def rows_a(q):
        return pl.ds(pl.multiple_of(q * group_a, group_a), group_a)

    def rows_b(q):
        return pl.ds(pl.multiple_of(q * group_b, group_b), group_b)

    def loop(lo, hi, body, unroll=1):
        def step(i, carry):
            body(i)
            return carry

        lax.fori_loop(lo, hi, step, 0, unroll=unroll)

    def remote(src, dst, name, k, seq, chan):
        return pltpu.make_async_remote_copy(
            src_ref=src,
            dst_ref=dst,
            send_sem=send_sem.at[first_sem[name] + k],
            recv_sem=recv_sem.at[first_sem[name] + k],
            device_id=(seq, chan),
            device_id_type=MESH,
        )

    barrier = pltpu.get_barrier_semaphore()

    def greet(seq, chan):
        pl.semaphore_signal(barrier, inc=1, device_id=(seq, chan), device_id_type=MESH)

    loop(1, nz, lambda k: greet(z_at(z_to(k)), c))
    loop(1, planes, lambda k: greet(plane_at(plane_to(k)), c))
    greet(nxt, c)
    greet(prv, c)
    greet(me, oc)

    mid_rows = pl.ds(STEP, rows)
    smalls = [
        pltpu.make_async_copy(src, dst, load_sem.at[4 + i])
        for i, (src, dst) in enumerate(
            (
                (track_hbm, track),
                (start_hbm, start),
                (end_hbm, end),
                (owner_hbm, owner),
                (gain_hbm, gain),
                (positive_hbm, positive),
            )
        )
    ]
    load_x = pltpu.make_async_copy(x_hbm, xp.at[c, mid_rows], load_sem.at[0])
    load_w = [
        pltpu.make_async_copy(w_hbm.at[k], w.at[k], load_sem.at[1 + k]) for k in range(TAPS)
    ]
    for copy in smalls:
        copy.start()
    load_x.start()
    for copy in smalls:
        copy.wait()
    own_track = track[...].astype(F32)
    track_a1[z] = own_track[:, 0:wide_a]
    track_b1[p] = own_track[:, wide_a:half]
    load_x.wait()
    pl.semaphore_wait(barrier, 3 + planes - 1 + nz - 1)

    piece = STEP // PIECES

    def to_next(i):
        src = pl.ds(rows + i * piece, piece)
        return remote(xp.at[c, src], xp.at[c, pl.ds(i * piece, piece)], "next", i, nxt, c)

    def to_prev(i):
        src = pl.ds(STEP + i * piece, piece)
        dst = pl.ds(STEP + rows + i * piece, piece)
        return remote(xp.at[c, src], xp.at[c, dst], "prev", i, prv, c)

    def core(side):
        return remote(xp.at[side, mid_rows], xp.at[side, mid_rows], "core", 0, me, oc)

    def left(side, i):
        some = pl.ds(i * piece, piece)
        return remote(xp.at[side, some], xp.at[side, some], "left", i, me, oc)

    def right(side, i):
        some = pl.ds(STEP + rows + i * piece, piece)
        return remote(xp.at[side, some], xp.at[side, some], "right", i, me, oc)

    for i in range(PIECES):
        to_next(i).start()
        to_prev(i).start()
    core(c).start()

    def gather_a1(buf, name, k, slot):
        return remote(buf.at[z], buf.at[slot], name, k, z_at(z_to(k)), c)

    def gather_b1(buf, name, k, slot):
        return remote(buf.at[p], buf.at[slot], name, k, plane_at(plane_to(k)), c)

    def gather_a2(buf, name, k, q):
        return remote(buf.at[rows_a(p)], buf.at[rows_a(q)], name, k, plane_at(plane_to(k)), c)

    def gather_b2(buf, name, k, q):
        return remote(buf.at[rows_b(z)], buf.at[rows_b(q)], name, k, z_at(z_to(k)), c)

    loop(1, nz, lambda k: gather_a1(track_a1, "track_a1", k, z).start())
    loop(1, planes, lambda k: gather_b1(track_b1, "track_b1", k, p).start())
    for copy in load_w:
        copy.start()

    first = start[...]
    last = end[...]
    slot_of = first_order(owner[...], dims, gl)
    spans = first.shape[1]
    base = me * rows - STEP

    def member_rows(i):
        at = pl.multiple_of(i * ROWS, ROWS)
        bins = base + at + lax.broadcasted_iota(jnp.int32, (ROWS, spans), 0)
        inside = (first <= bins) & (bins < last)
        member[pl.ds(at, ROWS), :] = jnp.where(inside, 1.0, 0.0).astype(BF16)

    def owner_rows(i):
        at = pl.multiple_of(i * ROWS, ROWS)
        gene = at + lax.broadcasted_iota(jnp.int32, (ROWS, spans), 0)
        own_hot[pl.ds(at, ROWS), :] = jnp.where(slot_of == gene, 1.0, 0.0).astype(BF16)

    def perm_rows(i):
        at = pl.multiple_of(i * ROWS, ROWS)
        down = at + lax.broadcasted_iota(jnp.int32, (ROWS, genes), 0)
        across = lax.broadcasted_iota(jnp.int32, (1, genes), 1)
        moved = second_from_first(at + lax.broadcasted_iota(jnp.int32, (ROWS, 1), 0), dims, gl)
        some = pl.ds(at, ROWS)
        perm[some, :] = jnp.where(across == moved, 1.0, 0.0).astype(BF16)
        across = second_from_first(across, dims, gl)
        perm_t[some, :] = jnp.where(across == down, 1.0, 0.0).astype(BF16)

    loop(0, genes // ROWS, owner_rows)
    loop(0, padded // ROWS, member_rows)

    def normed_rows(at):
        some = pl.ds(at, ROWS)
        x0 = xp[0, some, :].astype(F32)
        x1 = xp[1, some, :].astype(F32)
        total = jnp.sum(x0 * x0, axis=1, keepdims=True) + jnp.sum(x1 * x1, axis=1, keepdims=True)
        root = lax.rsqrt(total / width + EPS)
        return (x0, x1), root

    def gain_of(h):
        return gain[h * half : (h + 1) * half].reshape(1, half)

    def gelu(n):
        return 0.5 * n * (1.0 + jnp.tanh(GELU_A * (n + GELU_B * n * n * n)))

    def gelu_slope(n):
        t = jnp.tanh(GELU_A * (n + GELU_B * n * n * n))
        return 0.5 * (1.0 + t) + 0.5 * n * (1.0 - t * t) * (
            GELU_A * (1.0 + 3.0 * GELU_B * n * n)
        )

    def activate(lo, count, keep):
        def body(i):
            at = pl.multiple_of(lo + i * ROWS, ROWS)
            xs, root = normed_rows(at)
            for h in range(2):
                act[h, pl.ds(at, ROWS), :] = (gelu(xs[h] * root * gain_of(h)) * keep).astype(BF16)

        loop(0, count // ROWS, body)

    core(oc).wait_recv()
    activate(STEP, rows, 1.0)

    for copy in load_w:
        copy.wait()

    def tap(lo, count, k, some):
        return dot_nn(act[0, lo : lo + count, :], w[k, 0:half, some]) + dot_nn(
            act[1, lo : lo + count, :], w[k, half:width, some]
        )

    def centre_cols(i):
        some = pl.ds(pl.multiple_of(i * cols, cols), cols)
        acc[:, some] = xp[c, mid_rows, some].astype(F32) + tap(STEP, rows, 1, some)
        acc[0:STEP, some] += tap(rows, STEP, 2, some)
        acc[STEP:rows, some] += tap(STEP, STEP, 0, some)

    loop(0, half // cols, centre_cols)

    def gather_turn(a1, b1, a2, b2, name):
        def a_wait(k):
            gather_a1(a1, name + "_a1", k, z_from(k)).wait_recv()

        loop(1, nz, a_wait)
        for i in range(nz):
            tmp_a[i * gl : (i + 1) * gl, :] = a1[i, :, 0:wide_a]
        a2[rows_a(p), :] = tmp_a[...].astype(BF16)
        loop(1, planes, lambda k: gather_a2(a2, name + "_a2", k, p).start())

        def b_wait(k):
            gather_b1(b1, name + "_b1", k, plane_from(k)).wait_recv()

        loop(1, planes, b_wait)
        for i in range(planes):
            tmp_b[i * gl : (i + 1) * gl, :] = b1[i]
        b2[rows_b(z), :] = tmp_b[...].astype(BF16)
        loop(1, nz, lambda k: gather_b2(b2, name + "_b2", k, z).start())

    def gather_end_a(a2, name):
        def a_wait(k):
            gather_a2(a2, name + "_a2", k, plane_from(k)).wait_recv()

        loop(1, planes, a_wait)

    def gather_end_b(b2, name):
        def b_wait(k):
            gather_b2(b2, name + "_b2", k, z_from(k)).wait_recv()

        loop(1, nz, b_wait)

    gather_turn(track_a1, track_b1, trk_a, trk_raw, "track")

    keep_left = jnp.where(me > 0, 1.0, 0.0)
    keep_right = jnp.where(me < nseq - 1, 1.0, 0.0)
    for i in range(PIECES):
        to_next(i).wait_recv()
        left(c, i).start()
        to_prev(i).wait_recv()
        right(c, i).start()
        if i == 0:
            counts[...] = dot_nt(own_hot[...], member[mid_rows, :]).astype(BF16)
            loop(0, genes // ROWS, perm_rows)
        else:
            counts_b[...] = dot_nn(perm_t[...], counts[...]).astype(BF16)
        left(oc, i).wait_recv()
        activate(i * piece, piece, keep_left)
        right(oc, i).wait_recv()
        activate(STEP + rows + i * piece, piece, keep_right)

    def hidden_cols(i):
        some = slice(i * cols, (i + 1) * cols)
        hid[0:STEP, some] = (acc[0:STEP, some] + tap(0, STEP, 0, some)).astype(BF16)
        hid[STEP:rows, some] = (acc[STEP:rows, some] + tap(STEP + rows, STEP, 2, some)).astype(BF16)
        return hid[:, some]

    def pool_b1(k):
        q = z_to(k)
        return remote(send_b.at[rows_b(q)], recv_b.at[k], "pool_b1", k, z_at(q), c)

    def pool_a1(i, k):
        q = plane_to(k)
        return remote(
            send_a.at[i, rows_a(q)],
            recv_a.at[i, k],
            "pool_a1",
            i * planes + k,
            plane_at(q),
            c,
        )

    send_b[...] = dot_nn(counts_b[...], hidden_cols(2)).astype(BF16)
    loop(1, nz, lambda k: pool_b1(k).start())
    for i in range(2):
        send_a[i] = dot_nn(counts[...], hidden_cols(i)).astype(BF16)
        loop(1, planes, lambda k: pool_a1(i, k).start())

    def factor_rows(i):
        at = pl.multiple_of(i * ROWS, ROWS)
        some = pl.ds(at, ROWS)
        xs, root = normed_rows(STEP + at)
        mine = jnp.where(c == 0, xs[0], xs[1])
        g = jnp.where(c == 0, gain_of(0), gain_of(1))
        fac[some, :] = gelu_slope(mine * root * g) * (root * g)
        xq[some, :] = mine * (root * root / width)

    tile = min(256, genes)
    for i in range(genes // tile):
        some = slice(i * tile, (i + 1) * tile)
        counts_t[:, some] = dot_nt(member[...], own_hot[some, :]).astype(BF16)
    for i in range(genes // tile):
        some = slice(i * tile, (i + 1) * tile)
        counts_tb[:, some] = dot_nn(counts_t[...], perm[:, some]).astype(BF16)
    loop(0, rows // ROWS, factor_rows)

    def pool_b2(k):
        q = plane_to(k)
        return remote(send_b2.at[q], recv_b2.at[k], "pool_b2", k, plane_at(q), c)

    def pool_a2(k):
        q = z_to(k)
        return remote(send_a2.at[q], recv_a2.at[k], "pool_a2", k, z_at(q), c)

    def sum_b1(k, total):
        pool_b1(k).wait_recv()
        return total + recv_b[k].astype(F32)

    tmp_b[...] = lax.fori_loop(1, nz, sum_b1, send_b[rows_b(z), :].astype(F32))
    for i in range(planes):
        send_b2[i] = tmp_b[i * gl : (i + 1) * gl, :]
    loop(1, planes, lambda k: pool_b2(k).start())

    for i in range(2):

        def sum_a1(k, total):
            pool_a1(i, k).wait_recv()
            return total + recv_a[i, k].astype(F32)

        tmp_a[:, i * cols : (i + 1) * cols] = lax.fori_loop(
            1, planes, sum_a1, send_a[i, rows_a(p), :].astype(F32)
        )
    for i in range(nz):
        send_a2[i] = tmp_a[i * gl : (i + 1) * gl, :]
    loop(1, nz, lambda k: pool_a2(k).start())

    gather_end_a(trk_a, "track")
    gather_end_b(trk_raw, "track")
    trk_b[...] = dot_nn(perm[...], trk_raw[...]).astype(BF16)

    def sum_b2(k, total):
        pool_b2(k).wait_recv()
        return total + recv_b2[k]

    mine_b = lax.fori_loop(1, planes, sum_b2, send_b2[p])

    def sum_a2(k, total):
        pool_a2(k).wait_recv()
        return total + recv_a2[k]

    mine_a = lax.fori_loop(1, nz, sum_a2, send_a2[z])

    raw_part = dot_nt(mine_a.astype(BF16), trk_a[...]) + dot_nt(mine_b.astype(BF16), trk_b[...])
    sq_part = jnp.sum(mine_a * mine_a, axis=1, keepdims=True) + jnp.sum(
        mine_b * mine_b, axis=1, keepdims=True
    )
    mid_out[:, 0:genes] = raw_part
    mid_out[:, genes : genes + 128] = jnp.broadcast_to(sq_part, (gl, 128))
    mid = remote(mid_out, mid_in, "mid", 0, me, oc)
    mid.start()
    mid.wait_recv()
    both = mid_out[...] + mid_in[...]
    raw = both[:, 0:genes]
    scale = lax.rsqrt(both[:, genes : genes + 1] / width + EPS)
    unit = float(width) ** -0.5
    logits = raw * (scale * (INV_TEMP * unit))
    top = jnp.max(logits, axis=1, keepdims=True)
    log_total = top + jnp.log(jnp.sum(jnp.exp(logits - top), axis=1, keepdims=True))
    place = lax.broadcasted_iota(jnp.int32, (gl, genes), 0)
    want = jnp.zeros((gl, genes), jnp.int32)
    for i in range(gl):
        want = jnp.where(place == i, first_order(positive[i], dims, gl), want)
    hits = lax.broadcasted_iota(jnp.int32, (gl, genes), 1) == want
    weights = jnp.exp(logits - log_total)
    grad_logit = (LOSS_SCALE * (weights - jnp.where(hits, 1.0, 0.0))).astype(BF16)
    inner = INV_TEMP * jnp.sum(grad_logit.astype(F32) * raw, axis=1, keepdims=True)
    back = inner * scale * scale / width
    outer = unit * scale
    grad_b1[p] = outer * (INV_TEMP * dot_nn(grad_logit, trk_b[...]) - mine_b * back)
    loop(1, planes, lambda k: gather_b1(grad_b1, "grad_b1", k, p).start())
    per_gene = log_total - jnp.sum(jnp.where(hits, logits, 0.0), axis=1, keepdims=True)
    grad_a1[z, :, 0:wide_a] = outer * (INV_TEMP * dot_nn(grad_logit, trk_a[...]) - mine_a * back)
    grad_a1[z, :, wide_a : wide_a + 128] = jnp.broadcast_to(per_gene, (gl, 128))
    loop(1, nz, lambda k: gather_a1(grad_a1, "grad_a1", k, z).start())

    gather_turn(grad_a1, grad_b1, grad_a, grad_b, "grad")
    part = jnp.zeros((1, 128), F32)
    for i in range(nz):
        part = part + jnp.sum(grad_a1[i, :, wide_a : wide_a + 128], axis=0, keepdims=True)
    loss_out[...] = jnp.broadcast_to(part, (8, 128))
    loss_in[p] = loss_out[...]

    def loss_copy(k, q):
        return remote(loss_out, loss_in.at[q], "loss", k, plane_at(plane_to(k)), c)

    loop(1, planes, lambda k: loss_copy(k, p).start())

    gather_end_b(grad_b, "grad")
    hg[:, wide_a:half] = dot_nn(counts_tb[...], grad_b[...]).astype(BF16)
    gather_end_a(grad_a, "grad")
    for i in range(2):
        some = slice(i * cols, (i + 1) * cols)
        hg[:, some] = dot_nn(counts_t[...], grad_a[:, some]).astype(BF16)

    def activ_grad(h, i):
        wide = pl.ds(pl.multiple_of(h * half + i * cols, cols), cols)
        total = jnp.zeros((rows, cols), F32)
        for k in range(TAPS):
            lo = (TAPS - 1 - k) * STEP
            total = total + dot_nt(hg[lo : lo + rows, :], w[k, wide, :])
        return total

    def grad_copy(i):
        return remote(ga_send.at[i], ga_recv.at[i], "last", i, me, oc)

    for i in range(3):
        ga_send[i] = activ_grad(oc, i).astype(BF16)
        grad_copy(i).start()
    for i in range(3):
        ga_mine[:, i * cols : (i + 1) * cols] = activ_grad(c, i)

    def loss_wait(k):
        loss_copy(k, plane_from(k)).wait_recv()

    for i in range(PIECES):
        to_next(i).wait_send()
        to_prev(i).wait_send()
        left(c, i).wait_send()
        right(c, i).wait_send()
    core(c).wait_send()
    mid.wait_send()

    def z_sent(k):
        gather_a1(track_a1, "track_a1", k, z).wait_send()
        gather_b2(trk_raw, "track_b2", k, z).wait_send()
        pool_b1(k).wait_send()
        pool_a2(k).wait_send()
        gather_a1(grad_a1, "grad_a1", k, z).wait_send()
        gather_b2(grad_b, "grad_b2", k, z).wait_send()

    loop(1, nz, z_sent)

    def plane_sent(k):
        gather_b1(track_b1, "track_b1", k, p).wait_send()
        gather_a2(trk_a, "track_a2", k, p).wait_send()
        pool_a1(0, k).wait_send()
        pool_a1(1, k).wait_send()
        pool_b2(k).wait_send()
        gather_b1(grad_b1, "grad_b1", k, p).wait_send()
        gather_a2(grad_a, "grad_a2", k, p).wait_send()
        loss_copy(k, p).wait_send()

    loop(1, planes, plane_sent)
    for i in range(3):
        grad_copy(i).wait_recv()
    part_rows = rows // PIECES

    def dots_copy(i):
        return remote(dots.at[i], dots_in.at[i], "dots", i, me, oc)

    for i in range(PIECES):

        def weigh(j):
            at = pl.multiple_of(j * ROWS, ROWS)
            some = pl.ds(i * part_rows + at, ROWS)
            wide = pl.ds(STEP + i * part_rows + at, ROWS)
            got = jnp.concatenate([ga_recv[n, some, :] for n in range(3)], axis=1)
            v = fac[some, :] * (ga_mine[some, :] + got.astype(F32))
            out_v[some, :] = v
            inner = jnp.sum(xp[c, wide, :].astype(F32) * v, axis=1, keepdims=True)
            dots[i, pl.ds(at, ROWS), :] = jnp.broadcast_to(inner, (ROWS, 128))

        loop(0, part_rows // ROWS, weigh, unroll=True)
        dots_copy(i).start()
    loop(1, planes, loss_wait)
    total_loss = jnp.zeros((8, 128), F32)
    for i in range(planes):
        total_loss = total_loss + loss_in[i]
    loss_ref[...] = total_loss / genes
    for i in range(PIECES):
        dots_copy(i).wait_recv()

        def finish(j):
            at = pl.multiple_of(j * ROWS, ROWS)
            some = pl.ds(i * part_rows + at, ROWS)
            wide = pl.ds(STEP + i * part_rows + at, ROWS)
            inner = (dots[i, pl.ds(at, ROWS), :] + dots_in[i, pl.ds(at, ROWS), :])[:, 0:1]
            out_v[some, :] = out_v[some, :] + (hg[wide, :].astype(F32) - xq[some, :] * inner)

        loop(0, part_rows // ROWS, finish, unroll=True)
    for i in range(3):
        grad_copy(i).wait_send()
    for i in range(PIECES):
        dots_copy(i).wait_send()


def per_device(dims, stop, x, weight, gain, track, start, end, owner, positive):
    ny, nz, nx = dims
    nseq, planes = ny * nz * nx, ny * nx
    rows, half = x.shape
    gl = track.shape[0]
    genes, spans = gl * nseq, start.shape[0]
    group_a, group_b = gl * nz, gl * planes
    padded = rows + 2 * STEP
    cols = half // 3
    wide_a = 2 * cols
    copies = phases(dims)[1]
    dma = pltpu.SemaphoreType.DMA
    vmem = pl.BlockSpec(memory_space=pltpu.VMEM)
    scratch = [
        pltpu.VMEM((2 * half,), F32),
        pltpu.VMEM((gl, half), BF16),
        pltpu.VMEM((1, spans), jnp.int32),
        pltpu.VMEM((1, spans), jnp.int32),
        pltpu.VMEM((1, spans), jnp.int32),
        pltpu.SMEM((gl,), jnp.int32),
        pltpu.VMEM((2, padded, half), BF16),
        pltpu.VMEM((TAPS, 2 * half, half), BF16),
        pltpu.VMEM((2, padded, half), BF16),
        pltpu.VMEM((rows, half), F32),
        pltpu.VMEM((rows, half), F32),
        pltpu.VMEM((genes, spans), BF16),
        pltpu.VMEM((padded, spans), BF16),
        pltpu.VMEM((genes, rows), BF16),
        pltpu.VMEM((padded, genes), BF16),
        pltpu.VMEM((genes, rows), BF16),
        pltpu.VMEM((padded, genes), BF16),
        pltpu.VMEM((genes, genes), BF16),
        pltpu.VMEM((genes, genes), BF16),
        pltpu.VMEM((rows, half), F32),
        pltpu.VMEM((rows, half), BF16),
        pltpu.VMEM((2, genes, cols), BF16),
        pltpu.VMEM((2, planes, group_a, cols), BF16),
        pltpu.VMEM((genes, cols), BF16),
        pltpu.VMEM((nz, group_b, cols), BF16),
        pltpu.VMEM((group_a, wide_a), F32),
        pltpu.VMEM((group_b, cols), F32),
        pltpu.VMEM((nz, gl, wide_a), F32),
        pltpu.VMEM((nz, gl, wide_a), F32),
        pltpu.VMEM((planes, gl, cols), F32),
        pltpu.VMEM((planes, gl, cols), F32),
        pltpu.VMEM((nz, gl, wide_a), F32),
        pltpu.VMEM((planes, gl, cols), F32),
        pltpu.VMEM((genes, wide_a), BF16),
        pltpu.VMEM((genes, cols), BF16),
        pltpu.VMEM((genes, cols), BF16),
        pltpu.VMEM((gl, genes + 128), F32),
        pltpu.VMEM((gl, genes + 128), F32),
        pltpu.VMEM((nz, gl, wide_a + 128), F32),
        pltpu.VMEM((planes, gl, cols), F32),
        pltpu.VMEM((genes, wide_a), BF16),
        pltpu.VMEM((genes, cols), BF16),
        pltpu.VMEM((8, 128), F32),
        pltpu.VMEM((planes, 8, 128), F32),
        pltpu.VMEM((padded, half), BF16),
        pltpu.VMEM((rows, half), F32),
        pltpu.VMEM((3, rows, cols), BF16),
        pltpu.VMEM((3, rows, cols), BF16),
        pltpu.VMEM((PIECES, rows // PIECES, 128), F32),
        pltpu.VMEM((PIECES, rows // PIECES, 128), F32),
        dma((10,)),
        dma((copies,)),
        dma((copies,)),
    ]
    grad, loss = pl.pallas_call(
        functools.partial(kernel, dims, stop),
        out_shape=(
            jax.ShapeDtypeStruct((rows, half), F32),
            jax.ShapeDtypeStruct((8, 128), F32),
        ),
        in_specs=[pl.BlockSpec(memory_space=pltpu.HBM)] * 8,
        out_specs=(vmem, vmem),
        scratch_shapes=scratch,
        compiler_params=pltpu.CompilerParams(
            collective_id=0, has_side_effects=True, vmem_limit_bytes=48 * 1024 * 1024
        ),
    )(
        *(
            pltpu.with_memory_space_constraint(array, pltpu.HBM)
            for array in (
                x,
                weight,
                gain,
                track,
                start.reshape(1, -1),
                end.reshape(1, -1),
                owner.reshape(1, -1),
                positive,
            )
        )
    )
    return grad, loss[0, 0]


def solution(mesh, dims=(4, 8, 4), stop=99):
    return jax.shard_map(
        functools.partial(per_device, dims, stop),
        mesh=mesh,
        in_specs=(
            P("seq", "chan"),
            P(None, None, "chan"),
            P(),
            P("seq", "chan"),
            P(),
            P(),
            P(),
            P("seq"),
        ),
        out_specs=(P("seq", "chan"), P()),
        check_vma=False,
    )
```

```python
import functools

import jax
import jax.numpy as jnp
from jax import lax
from jax.experimental import pallas as pl
from jax.experimental.pallas import tpu as pltpu
from jax.sharding import PartitionSpec as P

STEP = 128
TAPS = 3
EPS = 1e-06
INV_TEMP = 2.0
LOSS_SCALE = 64.0
MESH = pl.DeviceIdType.MESH
F32 = jnp.float32
BF16 = jnp.bfloat16
ROWS = 32
PIECES = 2
CHUNKS = 2
GELU_A = 0.7978845608028654
GELU_B = 0.044715


def first_order(value, dims, genes_each):
    ny, nz, nx = dims
    place = lax.rem(value, genes_each)
    owner = lax.div(value, genes_each)
    x = lax.rem(owner, nx)
    z = lax.rem(lax.div(owner, nx), nz)
    y = lax.div(owner, nx * nz)
    return ((y * nx + x) * nz + z) * genes_each + place


def chunk_order(value, dims, genes_each):
    ny, nz, nx = dims
    each = genes_each // CHUNKS
    place = lax.rem(value, genes_each)
    return lax.div(place, each) * (ny * nz * nx * each) + first_order(
        lax.div(value, genes_each) * each + lax.rem(place, each), dims, each
    )


def second_from_chunk(row, dims, genes_each):
    ny, nz, nx = dims
    each = genes_each // CHUNKS
    part = ny * nz * nx * each
    return lax.div(row, part) * part + second_from_first(lax.rem(row, part), dims, each)


def second_from_first(row, dims, genes_each):
    ny, nz, nx = dims
    place = lax.rem(row, genes_each)
    z = lax.rem(lax.div(row, genes_each), nz)
    plane = lax.div(row, genes_each * nz)
    return (z * (ny * nx) + plane) * genes_each + place


def dot_nt(a, b):
    return lax.dot_general(a, b, (((1,), (1,)), ((), ())), preferred_element_type=F32)


def dot_nn(a, b):
    return jnp.dot(a, b, preferred_element_type=F32)


def phases():
    sizes = (
        ("core", 1),
        ("next", PIECES),
        ("prev", PIECES),
        ("left", PIECES),
        ("right", PIECES),
        ("mid", CHUNKS),
        ("last", 3),
        ("dots", PIECES),
        ("track_a1", 1),
        ("track_a2", 1),
        ("track_b1", 1),
        ("track_b2", 1),
        ("pool_b1", CHUNKS),
        ("pool_a1", CHUNKS),
        ("pool_a2", CHUNKS),
        ("pool_b2", CHUNKS),
        ("grad_a1", CHUNKS),
        ("grad_a2", CHUNKS),
        ("grad_b1", CHUNKS),
        ("grad_b2", CHUNKS),
        ("loss", 1),
    )
    at, total = {}, 0
    for name, size in sizes:
        at[name] = total
        total += size
    return at, total


def kernel(
    dims,
    stop,
    x_hbm,
    w_hbm,
    gain_hbm,
    track_hbm,
    start_hbm,
    end_hbm,
    owner_hbm,
    positive_hbm,
    out_v,
    loss_ref,
    gain,
    track,
    start,
    end,
    owner,
    positive,
    xp,
    w,
    act,
    fac,
    xq,
    own_hot,
    member,
    counts,
    counts_t,
    counts_b,
    counts_tb,
    perm,
    perm_t,
    perm_k,
    acc,
    hid,
    send_a,
    recv_a,
    send_b,
    recv_b,
    tmp_a,
    tmp_b,
    send_a2,
    recv_a2,
    send_b2,
    recv_b2,
    track_a1,
    track_b1,
    trk_a,
    trk_raw,
    trk_b,
    mid_out,
    mid_in,
    grad_a1,
    grad_b1,
    grad_a,
    grad_b,
    loss_out,
    loss_in,
    hg,
    hg_sum,
    ga_mine,
    ga_send,
    ga_recv,
    dots,
    dots_in,
    load_sem,
    send_sem,
    recv_sem,
):
    ny, nz, nx = dims
    nseq = ny * nz * nx
    planes = ny * nx
    rows, half = out_v.shape
    padded = rows + 2 * STEP
    width = 2 * half
    gl = track.shape[0]
    genes = gl * nseq
    group_a = gl * nz
    group_b = gl * planes
    each = gl // CHUNKS
    part_a = each * nz
    part_b = each * planes
    part = each * nseq
    cols = half // 3
    wide_a = 2 * cols
    first_sem, _ = phases()
    me = lax.axis_index("seq")
    c = lax.axis_index("chan")
    oc = 1 - c
    x = lax.rem(me, nx)
    z = lax.rem(lax.div(me, nx), nz)
    y = lax.div(me, nx * nz)
    p = y * nx + x
    nxt = lax.rem(me + 1, nseq)
    prv = lax.rem(me + nseq - 1, nseq)

    def plane_at(q):
        return (lax.div(q, nx) * nz + z) * nx + lax.rem(q, nx)

    def plane_to(k):
        return lax.rem(p + k, planes)

    def plane_from(k):
        return lax.rem(p + planes - k, planes)

    def z_at(q):
        return (y * nz + q) * nx + x

    def z_to(k):
        return lax.rem(z + k, nz)

    def z_from(k):
        return lax.rem(z + nz - k, nz)

    def rows_a(q):
        return pl.ds(pl.multiple_of(q * group_a, group_a), group_a)

    def rows_b(q):
        return pl.ds(pl.multiple_of(q * group_b, group_b), group_b)

    def chunk_a(n, q):
        return pl.ds(pl.multiple_of(n * part + q * part_a, part_a), part_a)

    def chunk_b(n, q):
        return pl.ds(pl.multiple_of(n * part + q * part_b, part_b), part_b)

    def chunk_rows(n):
        return slice(n * part, (n + 1) * part)

    def loop(lo, hi, body, unroll=1):
        def step(i, carry):
            body(i)
            return carry

        lax.fori_loop(lo, hi, step, 0, unroll=unroll)

    def remote(src, dst, name, k, seq, chan):
        return pltpu.make_async_remote_copy(
            src_ref=src,
            dst_ref=dst,
            send_sem=send_sem.at[first_sem[name] + k],
            recv_sem=recv_sem.at[first_sem[name] + k],
            device_id=(seq, chan),
            device_id_type=MESH,
        )

    barrier = pltpu.get_barrier_semaphore()

    def greet(seq, chan):
        pl.semaphore_signal(barrier, inc=1, device_id=(seq, chan), device_id_type=MESH)

    loop(1, nz, lambda k: greet(z_at(z_to(k)), c))
    loop(1, planes, lambda k: greet(plane_at(plane_to(k)), c))
    greet(nxt, c)
    greet(prv, c)
    greet(me, oc)

    def all_in(of, name, k=0):
        pltpu.make_async_copy(of, of, recv_sem.at[first_sem[name] + k]).wait()

    def all_out(of, name, k=0):
        pltpu.make_async_copy(of, of, send_sem.at[first_sem[name] + k]).wait()

    others_z = pl.ds(0, nz - 1)
    others_p = pl.ds(0, planes - 1)

    mid_rows = pl.ds(STEP, rows)
    smalls = [
        pltpu.make_async_copy(src, dst, load_sem.at[4 + i])
        for i, (src, dst) in enumerate(
            (
                (track_hbm, track),
                (start_hbm, start),
                (end_hbm, end),
                (owner_hbm, owner),
                (gain_hbm, gain),
                (positive_hbm, positive),
            )
        )
    ]
    load_x = pltpu.make_async_copy(x_hbm, xp.at[c, mid_rows], load_sem.at[0])
    load_w = [
        pltpu.make_async_copy(w_hbm.at[k], w.at[k], load_sem.at[1 + k]) for k in range(TAPS)
    ]
    for copy in smalls:
        copy.start()
    load_x.start()
    pl.semaphore_wait(barrier, 3 + planes - 1 + nz - 1)

    piece = STEP // PIECES

    def to_next(i):
        src = pl.ds(rows - STEP + i * piece, piece)
        return remote(x_hbm.at[src], xp.at[c, pl.ds(i * piece, piece)], "next", i, nxt, c)

    def to_prev(i):
        src = pl.ds(i * piece, piece)
        dst = pl.ds(STEP + rows + i * piece, piece)
        return remote(x_hbm.at[src], xp.at[c, dst], "prev", i, prv, c)

    def core(side):
        return remote(x_hbm, xp.at[side, mid_rows], "core", 0, me, oc)

    def left(side, i):
        some = pl.ds(i * piece, piece)
        return remote(xp.at[side, some], xp.at[side, some], "left", i, me, oc)

    def right(side, i):
        some = pl.ds(STEP + rows + i * piece, piece)
        return remote(xp.at[side, some], xp.at[side, some], "right", i, me, oc)

    core(c).start()
    to_next(0).start()
    to_prev(0).start()

    def gather_a1(buf, name, k, slot):
        return remote(buf.at[z], buf.at[slot], name, 0, z_at(z_to(k)), c)

    def gather_b1(buf, name, k, slot):
        return remote(buf.at[p], buf.at[slot], name, 0, plane_at(plane_to(k)), c)

    def gather_a2(buf, name, k, q):
        return remote(buf.at[rows_a(p)], buf.at[rows_a(q)], name, 0, plane_at(plane_to(k)), c)

    def gather_b2(buf, name, k, q):
        return remote(buf.at[rows_b(z)], buf.at[rows_b(q)], name, 0, z_at(z_to(k)), c)

    for copy in smalls:
        copy.wait()
    own_track = track[...].astype(F32)
    track_b1[p] = own_track[:, wide_a:half]
    loop(1, planes, lambda k: gather_b1(track_b1, "track_b1", k, p).start())
    track_a1[z] = own_track[:, 0:wide_a]
    loop(1, nz, lambda k: gather_a1(track_a1, "track_a1", k, z).start())
    to_next(1).start()
    to_prev(1).start()
    for copy in load_w:
        copy.start()

    first = start[...]
    last = end[...]
    slot_of = chunk_order(owner[...], dims, gl)
    spans = first.shape[1]
    base = me * rows - STEP

    def member_rows(i):
        at = pl.multiple_of(i * ROWS, ROWS)
        bins = base + at + lax.broadcasted_iota(jnp.int32, (ROWS, spans), 0)
        inside = (first <= bins) & (bins < last)
        member[pl.ds(at, ROWS), :] = jnp.where(inside, 1.0, 0.0).astype(BF16)

    def owner_rows(i):
        at = pl.multiple_of(i * ROWS, ROWS)
        gene = at + lax.broadcasted_iota(jnp.int32, (ROWS, spans), 0)
        own_hot[pl.ds(at, ROWS), :] = jnp.where(slot_of == gene, 1.0, 0.0).astype(BF16)

    def perm_rows(i):
        at = pl.multiple_of(i * ROWS, ROWS)
        down = at + lax.broadcasted_iota(jnp.int32, (ROWS, genes), 0)
        across = lax.broadcasted_iota(jnp.int32, (1, genes), 1)
        row = at + lax.broadcasted_iota(jnp.int32, (ROWS, 1), 0)
        some = pl.ds(at, ROWS)
        moved = second_from_first(row, dims, gl)
        perm_k[some, :] = jnp.where(across == moved, 1.0, 0.0).astype(BF16)
        moved = second_from_chunk(row, dims, gl)
        perm[some, :] = jnp.where(across == moved, 1.0, 0.0).astype(BF16)
        across = second_from_chunk(across, dims, gl)
        perm_t[some, :] = jnp.where(across == down, 1.0, 0.0).astype(BF16)

    loop(0, genes // ROWS, owner_rows)
    loop(0, padded // ROWS, member_rows)

    def normed_rows(at):
        some = pl.ds(at, ROWS)
        x0 = xp[0, some, :].astype(F32)
        x1 = xp[1, some, :].astype(F32)
        total = jnp.sum(x0 * x0, axis=1, keepdims=True) + jnp.sum(x1 * x1, axis=1, keepdims=True)
        root = lax.rsqrt(total / width + EPS)
        return (x0, x1), root

    def gain_of(h):
        return gain[h * half : (h + 1) * half].reshape(1, half)

    def gelu(n):
        return 0.5 * n * (1.0 + jnp.tanh(GELU_A * (n + GELU_B * n * n * n)))

    def gelu_slope(n):
        t = jnp.tanh(GELU_A * (n + GELU_B * n * n * n))
        return 0.5 * (1.0 + t) + 0.5 * n * (1.0 - t * t) * (
            GELU_A * (1.0 + 3.0 * GELU_B * n * n)
        )

    def activate(lo, count, keep):
        def body(i):
            at = pl.multiple_of(lo + i * ROWS, ROWS)
            xs, root = normed_rows(at)
            for h in range(2):
                act[h, pl.ds(at, ROWS), :] = (gelu(xs[h] * root * gain_of(h)) * keep).astype(BF16)

        loop(0, count // ROWS, body)

    load_x.wait()
    core(oc).wait_recv()
    activate(STEP, rows, 1.0)

    for copy in load_w:
        copy.wait()

    def tap(lo, count, k, some):
        return dot_nn(act[0, lo : lo + count, :], w[k, 0:half, some]) + dot_nn(
            act[1, lo : lo + count, :], w[k, half:width, some]
        )

    def centre_cols(i):
        some = pl.ds(pl.multiple_of(i * cols, cols), cols)
        acc[:, some] = xp[c, mid_rows, some].astype(F32) + tap(STEP, rows, 1, some)
        acc[0:STEP, some] += tap(rows, STEP, 2, some)
        acc[STEP:rows, some] += tap(STEP, STEP, 0, some)

    loop(0, half // cols, centre_cols)

    def gather_turn(a1, b1, a2, b2, name):
        all_in(a1.at[others_z], name + "_a1")
        for i in range(nz):
            tmp_a[i * gl : (i + 1) * gl, :] = a1[i, :, 0:wide_a]
        a2[rows_a(p), :] = tmp_a[...].astype(BF16)
        loop(1, planes, lambda k: gather_a2(a2, name + "_a2", k, p).start())

        all_in(b1.at[others_p], name + "_b1")
        for i in range(planes):
            tmp_b[i * gl : (i + 1) * gl, :] = b1[i]
        b2[rows_b(z), :] = tmp_b[...].astype(BF16)
        loop(1, nz, lambda k: gather_b2(b2, name + "_b2", k, z).start())

    def gather_end_a(a2, name):
        all_in(a2.at[pl.ds(0, (planes - 1) * group_a)], name + "_a2")

    def gather_end_b(b2, name):
        all_in(b2.at[pl.ds(0, (nz - 1) * group_b)], name + "_b2")

    gather_turn(track_a1, track_b1, trk_a, trk_raw, "track")

    keep_left = jnp.where(me > 0, 1.0, 0.0)
    keep_right = jnp.where(me < nseq - 1, 1.0, 0.0)
    for i in range(PIECES):
        to_next(i).wait_recv()
        left(c, i).start()
        to_prev(i).wait_recv()
        right(c, i).start()
        if i == 0:
            counts[...] = dot_nt(own_hot[...], member[mid_rows, :]).astype(BF16)
            loop(0, genes // ROWS, perm_rows)
        else:
            counts_b[...] = dot_nn(perm_t[...], counts[...]).astype(BF16)
        left(oc, i).wait_recv()
        activate(i * piece, piece, keep_left)
        right(oc, i).wait_recv()
        activate(STEP + rows + i * piece, piece, keep_right)

    def hidden_cols(i):
        some = slice(i * cols, (i + 1) * cols)
        hid[0:STEP, some] = (acc[0:STEP, some] + tap(0, STEP, 0, some)).astype(BF16)
        hid[STEP:rows, some] = (acc[STEP:rows, some] + tap(STEP + rows, STEP, 2, some)).astype(BF16)

    def pool_b1(n, k):
        q = z_to(k)
        return remote(send_b.at[chunk_b(n, q)], recv_b.at[n, k], "pool_b1", n, z_at(q), c)

    def pool_a1(n, k):
        q = plane_to(k)
        return remote(
            send_a.at[chunk_a(n, q)], recv_a.at[n, k], "pool_a1", n, plane_at(q), c
        )

    for n in range(CHUNKS):
        some = chunk_rows(n)
        for i in range(2):
            tile = slice(i * cols, (i + 1) * cols)
            if n == 0:
                hidden_cols(i)
            send_a[some, tile] = dot_nn(counts[some, :], hid[:, tile]).astype(BF16)
        loop(1, planes, lambda k: pool_a1(n, k).start())
        if n == 0:
            hidden_cols(2)
        send_b[some, :] = dot_nn(counts_b[some, :], hid[:, wide_a:half]).astype(BF16)
        loop(1, nz, lambda k: pool_b1(n, k).start())

    def factor_rows(i):
        at = pl.multiple_of(i * ROWS, ROWS)
        some = pl.ds(at, ROWS)
        xs, root = normed_rows(STEP + at)
        mine = jnp.where(c == 0, xs[0], xs[1])
        g = jnp.where(c == 0, gain_of(0), gain_of(1))
        fac[some, :] = gelu_slope(mine * root * g) * (root * g)
        xq[some, :] = mine * (root * root / width)

    tile = min(256, genes)
    for i in range(genes // tile):
        some = slice(i * tile, (i + 1) * tile)
        counts_t[:, some] = dot_nt(member[...], own_hot[some, :]).astype(BF16)
    for i in range(genes // tile):
        some = slice(i * tile, (i + 1) * tile)
        counts_tb[:, some] = dot_nn(counts_t[...], perm[:, some]).astype(BF16)
    loop(0, rows // ROWS, factor_rows)

    def pool_b2(n, k):
        q = plane_to(k)
        return remote(
            send_b2.at[n, q], recv_b2.at[n, k], "pool_b2", n, plane_at(q), c
        )

    def pool_a2(n, k):
        q = z_to(k)
        return remote(send_a2.at[n, q], recv_a2.at[n, k], "pool_a2", n, z_at(q), c)

    for n in range(CHUNKS):

        part_sum = send_a[chunk_a(n, p), :].astype(F32)
        all_in(recv_a.at[n, others_p], "pool_a1", n)
        for k in range(1, planes):
            part_sum = part_sum + recv_a[n, k].astype(F32)
        for i in range(nz):
            send_a2[n, i] = part_sum[i * each : (i + 1) * each, :]
        loop(1, nz, lambda k: pool_a2(n, k).start())

        part_sum = send_b[chunk_b(n, z), :].astype(F32)
        all_in(recv_b.at[n, others_z], "pool_b1", n)
        for k in range(1, nz):
            part_sum = part_sum + recv_b[n, k].astype(F32)
        for i in range(planes):
            send_b2[n, i] = part_sum[i * each : (i + 1) * each, :]
        loop(1, planes, lambda k: pool_b2(n, k).start())

    gather_end_a(trk_a, "track")
    gather_end_b(trk_raw, "track")
    trk_b[...] = dot_nn(perm_k[...], trk_raw[...]).astype(BF16)

    def grad_a1_copy(n, k, slot):
        return remote(
            grad_a1.at[n, z], grad_a1.at[n, slot], "grad_a1", n, z_at(z_to(k)), c
        )

    def grad_b1_copy(n, k, slot):
        return remote(
            grad_b1.at[n, p],
            grad_b1.at[n, slot],
            "grad_b1",
            n,
            plane_at(plane_to(k)),
            c,
        )

    def grad_a2_copy(n, k, q):
        return remote(
            grad_a.at[chunk_a(n, p)],
            grad_a.at[chunk_a(n, q)],
            "grad_a2",
            n,
            plane_at(plane_to(k)),
            c,
        )

    def grad_b2_copy(n, k, q):
        return remote(
            grad_b.at[chunk_b(n, z)],
            grad_b.at[chunk_b(n, q)],
            "grad_b2",
            n,
            z_at(z_to(k)),
            c,
        )

    def mid_copy(n):
        return remote(mid_out.at[n], mid_in.at[n], "mid", n, me, oc)

    for n in range(CHUNKS):

        mine_b = send_b2[n, p]
        all_in(recv_b2.at[n, others_p], "pool_b2", n)
        for k in range(1, planes):
            mine_b = mine_b + recv_b2[n, k]
        mine_a = send_a2[n, z]
        all_in(recv_a2.at[n, others_z], "pool_a2", n)
        for k in range(1, nz):
            mine_a = mine_a + recv_a2[n, k]
        raw_part = dot_nt(mine_a.astype(BF16), trk_a[...]) + dot_nt(
            mine_b.astype(BF16), trk_b[...]
        )
        sq_part = jnp.sum(mine_a * mine_a, axis=1, keepdims=True) + jnp.sum(
            mine_b * mine_b, axis=1, keepdims=True
        )
        mid_out[n, :, 0:genes] = raw_part
        mid_out[n, :, genes : genes + 128] = jnp.broadcast_to(sq_part, (each, 128))
        mid_copy(n).start()
        mid_copy(n).wait_recv()
        both = mid_out[n] + mid_in[n]
        raw = both[:, 0:genes]
        scale = lax.rsqrt(both[:, genes : genes + 1] / width + EPS)
        unit = float(width) ** -0.5
        logits = raw * (scale * (INV_TEMP * unit))
        top = jnp.max(logits, axis=1, keepdims=True)
        log_total = top + jnp.log(jnp.sum(jnp.exp(logits - top), axis=1, keepdims=True))
        place = lax.broadcasted_iota(jnp.int32, (each, genes), 0)
        want = jnp.zeros((each, genes), jnp.int32)
        for i in range(each):
            want = jnp.where(place == i, first_order(positive[n * each + i], dims, gl), want)
        hits = lax.broadcasted_iota(jnp.int32, (each, genes), 1) == want
        weights = jnp.exp(logits - log_total)
        grad_logit = (LOSS_SCALE * (weights - jnp.where(hits, 1.0, 0.0))).astype(BF16)
        inner = INV_TEMP * jnp.sum(grad_logit.astype(F32) * raw, axis=1, keepdims=True)
        back = inner * scale * scale / width
        outer = unit * scale
        per_gene = log_total - jnp.sum(jnp.where(hits, logits, 0.0), axis=1, keepdims=True)
        grad_a1[n, z, :, 0:wide_a] = outer * (
            INV_TEMP * dot_nn(grad_logit, trk_a[...]) - mine_a * back
        )
        grad_a1[n, z, :, wide_a : wide_a + 128] = jnp.broadcast_to(per_gene, (each, 128))
        loop(1, nz, lambda k: grad_a1_copy(n, k, z).start())
        grad_b1[n, p] = outer * (INV_TEMP * dot_nn(grad_logit, trk_b[...]) - mine_b * back)
        loop(1, planes, lambda k: grad_b1_copy(n, k, p).start())

    for n in range(CHUNKS):

        all_in(grad_b1.at[n, others_p], "grad_b1", n)
        for i in range(planes):
            tmp_b[i * each : (i + 1) * each, :] = grad_b1[n, i]
        grad_b[chunk_b(n, z), :] = tmp_b[0:part_b, :].astype(BF16)
        loop(1, nz, lambda k: grad_b2_copy(n, k, z).start())

        all_in(grad_a1.at[n, others_z], "grad_a1", n)
        for i in range(nz):
            tmp_a[i * each : (i + 1) * each, :] = grad_a1[n, i, :, 0:wide_a]
        grad_a[chunk_a(n, p), :] = tmp_a[0:part_a, :].astype(BF16)
        loop(1, planes, lambda k: grad_a2_copy(n, k, p).start())

    some_loss = jnp.zeros((1, 128), F32)
    for n in range(CHUNKS):
        for i in range(nz):
            some_loss = some_loss + jnp.sum(
                grad_a1[n, i, :, wide_a : wide_a + 128], axis=0, keepdims=True
            )
    loss_out[...] = jnp.broadcast_to(some_loss, (8, 128))
    loss_in[p] = loss_out[...]

    def loss_copy(k, q):
        return remote(loss_out, loss_in.at[q], "loss", 0, plane_at(plane_to(k)), c)

    loop(1, planes, lambda k: loss_copy(k, p).start())

    for n in range(CHUNKS):
        some = chunk_rows(n)

        all_in(grad_b.at[pl.ds(0, (nz - 1) * part_b)], "grad_b2", n)
        for i in (2, 0, 1):
            tile = slice(i * cols, (i + 1) * cols)
            if i == 2:
                total = dot_nn(counts_tb[:, some], grad_b[some, :])
            else:
                if i == 0:
                    all_in(grad_a.at[pl.ds(0, (planes - 1) * part_a)], "grad_a2", n)
                total = dot_nn(counts_t[:, some], grad_a[some, tile])
            if n > 0:
                total = total + hg_sum[:, tile]
            if n < CHUNKS - 1:
                hg_sum[:, tile] = total
            else:
                hg[:, tile] = total.astype(BF16)

    def activ_grad(h, i):
        wide = pl.ds(pl.multiple_of(h * half + i * cols, cols), cols)
        total = jnp.zeros((rows, cols), F32)
        for k in range(TAPS):
            lo = (TAPS - 1 - k) * STEP
            total = total + dot_nt(hg[lo : lo + rows, :], w[k, wide, :])
        return total

    def grad_copy(i):
        return remote(ga_send.at[i], ga_recv.at[i], "last", i, me, oc)

    for i in range(3):
        ga_send[i] = activ_grad(oc, i).astype(BF16)
        grad_copy(i).start()
    for i in range(3):
        ga_mine[:, i * cols : (i + 1) * cols] = activ_grad(c, i)

    for i in range(3):
        grad_copy(i).wait_recv()
    part_rows = rows // PIECES

    def dots_copy(i):
        return remote(dots.at[i], dots_in.at[i], "dots", i, me, oc)

    for i in range(PIECES):

        def weigh(j):
            at = pl.multiple_of(j * ROWS, ROWS)
            some = pl.ds(i * part_rows + at, ROWS)
            wide = pl.ds(STEP + i * part_rows + at, ROWS)
            got = jnp.concatenate([ga_recv[n, some, :] for n in range(3)], axis=1)
            v = fac[some, :] * (ga_mine[some, :] + got.astype(F32))
            out_v[some, :] = v
            inner = jnp.sum(xp[c, wide, :].astype(F32) * v, axis=1, keepdims=True)
            dots[i, pl.ds(at, ROWS), :] = jnp.broadcast_to(inner, (ROWS, 128))

        loop(0, part_rows // ROWS, weigh, unroll=True)
        dots_copy(i).start()
    all_in(loss_in.at[others_p], "loss")
    total_loss = jnp.zeros((8, 128), F32)
    for i in range(planes):
        total_loss = total_loss + loss_in[i]
    loss_ref[...] = total_loss / genes
    for i in range(PIECES):
        dots_copy(i).wait_recv()

        def finish(j):
            at = pl.multiple_of(j * ROWS, ROWS)
            some = pl.ds(i * part_rows + at, ROWS)
            wide = pl.ds(STEP + i * part_rows + at, ROWS)
            inner = (dots[i, pl.ds(at, ROWS), :] + dots_in[i, pl.ds(at, ROWS), :])[:, 0:1]
            out_v[some, :] = out_v[some, :] + (hg[wide, :].astype(F32) - xq[some, :] * inner)

        loop(0, part_rows // ROWS, finish, unroll=True)
    for i in range(PIECES):
        to_next(i).wait_send()
        to_prev(i).wait_send()
        left(c, i).wait_send()
        right(c, i).wait_send()
    core(c).wait_send()

    all_out(track_a1.at[others_z], "track_a1")
    all_out(track_b1.at[others_p], "track_b1")
    all_out(trk_a.at[pl.ds(0, (planes - 1) * group_a)], "track_a2")
    all_out(trk_raw.at[pl.ds(0, (nz - 1) * group_b)], "track_b2")
    all_out(loss_in.at[others_p], "loss")
    for n in range(CHUNKS):
        all_out(recv_a.at[n, others_p], "pool_a1", n)
        all_out(recv_b.at[n, others_z], "pool_b1", n)
        all_out(recv_a2.at[n, others_z], "pool_a2", n)
        all_out(recv_b2.at[n, others_p], "pool_b2", n)
        all_out(grad_a1.at[n, others_z], "grad_a1", n)
        all_out(grad_b1.at[n, others_p], "grad_b1", n)
        all_out(grad_a.at[pl.ds(0, (planes - 1) * part_a)], "grad_a2", n)
        all_out(grad_b.at[pl.ds(0, (nz - 1) * part_b)], "grad_b2", n)
    for n in range(CHUNKS):
        mid_copy(n).wait_send()
    for i in range(3):
        grad_copy(i).wait_send()
    for i in range(PIECES):
        dots_copy(i).wait_send()


def per_device(dims, stop, x, weight, gain, track, start, end, owner, positive):
    ny, nz, nx = dims
    nseq, planes = ny * nz * nx, ny * nx
    rows, half = x.shape
    gl = track.shape[0]
    genes, spans = gl * nseq, start.shape[0]
    group_a, group_b = gl * nz, gl * planes
    padded = rows + 2 * STEP
    each = gl // CHUNKS
    cols = half // 3
    wide_a = 2 * cols
    copies = phases()[1]
    dma = pltpu.SemaphoreType.DMA
    vmem = pl.BlockSpec(memory_space=pltpu.VMEM)
    scratch = [
        pltpu.VMEM((2 * half,), F32),
        pltpu.VMEM((gl, half), BF16),
        pltpu.VMEM((1, spans), jnp.int32),
        pltpu.VMEM((1, spans), jnp.int32),
        pltpu.VMEM((1, spans), jnp.int32),
        pltpu.SMEM((gl,), jnp.int32),
        pltpu.VMEM((2, padded, half), BF16),
        pltpu.VMEM((TAPS, 2 * half, half), BF16),
        pltpu.VMEM((2, padded, half), BF16),
        pltpu.VMEM((rows, half), F32),
        pltpu.VMEM((rows, half), F32),
        pltpu.VMEM((genes, spans), BF16),
        pltpu.VMEM((padded, spans), BF16),
        pltpu.VMEM((genes, rows), BF16),
        pltpu.VMEM((padded, genes), BF16),
        pltpu.VMEM((genes, rows), BF16),
        pltpu.VMEM((padded, genes), BF16),
        pltpu.VMEM((genes, genes), BF16),
        pltpu.VMEM((genes, genes), BF16),
        pltpu.VMEM((genes, genes), BF16),
        pltpu.VMEM((rows, half), F32),
        pltpu.VMEM((rows, half), BF16),
        pltpu.VMEM((genes, wide_a), BF16),
        pltpu.VMEM((CHUNKS, planes, each * nz, wide_a), BF16),
        pltpu.VMEM((genes, cols), BF16),
        pltpu.VMEM((CHUNKS, nz, each * planes, cols), BF16),
        pltpu.VMEM((group_a, wide_a), F32),
        pltpu.VMEM((group_b, cols), F32),
        pltpu.VMEM((CHUNKS, nz, each, wide_a), F32),
        pltpu.VMEM((CHUNKS, nz, each, wide_a), F32),
        pltpu.VMEM((CHUNKS, planes, each, cols), F32),
        pltpu.VMEM((CHUNKS, planes, each, cols), F32),
        pltpu.VMEM((nz, gl, wide_a), F32),
        pltpu.VMEM((planes, gl, cols), F32),
        pltpu.VMEM((genes, wide_a), BF16),
        pltpu.VMEM((genes, cols), BF16),
        pltpu.VMEM((genes, cols), BF16),
        pltpu.VMEM((CHUNKS, each, genes + 128), F32),
        pltpu.VMEM((CHUNKS, each, genes + 128), F32),
        pltpu.VMEM((CHUNKS, nz, each, wide_a + 128), F32),
        pltpu.VMEM((CHUNKS, planes, each, cols), F32),
        pltpu.VMEM((genes, wide_a), BF16),
        pltpu.VMEM((genes, cols), BF16),
        pltpu.VMEM((8, 128), F32),
        pltpu.VMEM((planes, 8, 128), F32),
        pltpu.VMEM((padded, half), BF16),
        pltpu.VMEM((padded, half), F32),
        pltpu.VMEM((rows, half), F32),
        pltpu.VMEM((3, rows, cols), BF16),
        pltpu.VMEM((3, rows, cols), BF16),
        pltpu.VMEM((PIECES, rows // PIECES, 128), F32),
        pltpu.VMEM((PIECES, rows // PIECES, 128), F32),
        dma((10,)),
        dma((copies,)),
        dma((copies,)),
    ]
    grad, loss = pl.pallas_call(
        functools.partial(kernel, dims, stop),
        out_shape=(
            jax.ShapeDtypeStruct((rows, half), F32),
            jax.ShapeDtypeStruct((8, 128), F32),
        ),
        in_specs=[pl.BlockSpec(memory_space=pltpu.HBM)] * 8,
        out_specs=(vmem, vmem),
        scratch_shapes=scratch,
        compiler_params=pltpu.CompilerParams(
            collective_id=0, has_side_effects=True, vmem_limit_bytes=48 * 1024 * 1024
        ),
    )(
        *(
            pltpu.with_memory_space_constraint(array, pltpu.HBM)
            for array in (
                x,
                weight,
                gain,
                track,
                start.reshape(1, -1),
                end.reshape(1, -1),
                owner.reshape(1, -1),
                positive,
            )
        )
    )
    return grad, loss[0, 0]


def solution(mesh, dims=(4, 8, 4), stop=99):
    return jax.shard_map(
        functools.partial(per_device, dims, stop),
        mesh=mesh,
        in_specs=(
            P("seq", "chan"),
            P(None, None, "chan"),
            P(),
            P("seq", "chan"),
            P(),
            P(),
            P(),
            P("seq"),
        ),
        out_specs=(P("seq", "chan"), P()),
        check_vma=False,
    )
```

```python
import functools

import jax
import jax.numpy as jnp
from jax import lax
from jax.experimental import pallas as pl
from jax.experimental.pallas import tpu as pltpu
from jax.sharding import PartitionSpec as P

STEP = 128
TAPS = 3
EPS = 1e-06
INV_TEMP = 2.0
LOSS_SCALE = 64.0
MESH = pl.DeviceIdType.MESH
F32 = jnp.float32
BF16 = jnp.bfloat16
ROWS = 32
PIECES = 2
CHUNKS = 2
GELU_A = 0.7978845608028654
GELU_B = 0.044715


def first_order(value, dims, genes_each):
    ny, nz, nx = dims
    place = lax.rem(value, genes_each)
    owner = lax.div(value, genes_each)
    x = lax.rem(owner, nx)
    z = lax.rem(lax.div(owner, nx), nz)
    y = lax.div(owner, nx * nz)
    return ((y * nx + x) * nz + z) * genes_each + place


def chunk_order(value, dims, genes_each):
    ny, nz, nx = dims
    each = genes_each // CHUNKS
    place = lax.rem(value, genes_each)
    return lax.div(place, each) * (ny * nz * nx * each) + first_order(
        lax.div(value, genes_each) * each + lax.rem(place, each), dims, each
    )


def second_from_chunk(row, dims, genes_each):
    ny, nz, nx = dims
    each = genes_each // CHUNKS
    part = ny * nz * nx * each
    return lax.div(row, part) * part + second_from_first(lax.rem(row, part), dims, each)


def second_from_first(row, dims, genes_each):
    ny, nz, nx = dims
    place = lax.rem(row, genes_each)
    z = lax.rem(lax.div(row, genes_each), nz)
    plane = lax.div(row, genes_each * nz)
    return (z * (ny * nx) + plane) * genes_each + place


def dot_nt(a, b):
    return lax.dot_general(a, b, (((1,), (1,)), ((), ())), preferred_element_type=F32)


def dot_nn(a, b):
    return jnp.dot(a, b, preferred_element_type=F32)


def phases():
    sizes = (
        ("core", 1),
        ("next", PIECES),
        ("prev", PIECES),
        ("left", PIECES),
        ("right", PIECES),
        ("mid", CHUNKS),
        ("last", 3),
        ("dots", PIECES),
        ("track_a1", 1),
        ("track_a2", 1),
        ("track_b1", 1),
        ("track_b2", 1),
        ("pool_b1", CHUNKS),
        ("pool_a1", CHUNKS),
        ("pool_a2", CHUNKS),
        ("pool_b2", CHUNKS),
        ("grad_a1", CHUNKS),
        ("grad_a2", CHUNKS),
        ("grad_b1", CHUNKS),
        ("grad_b2", CHUNKS),
        ("loss", 1),
    )
    at, total = {}, 0
    for name, size in sizes:
        at[name] = total
        total += size
    return at, total


def kernel(
    dims,
    stop,
    x_hbm,
    w_hbm,
    gain_hbm,
    track_hbm,
    start_hbm,
    end_hbm,
    owner_hbm,
    positive_hbm,
    out_v,
    loss_ref,
    gain,
    track,
    start,
    end,
    owner,
    positive,
    xp,
    w,
    act,
    fac,
    xq,
    own_hot,
    member,
    counts,
    counts_t,
    counts_b,
    counts_tb,
    perm,
    perm_t,
    perm_k,
    acc,
    hid,
    send_a,
    recv_a,
    send_b,
    recv_b,
    tmp_a,
    tmp_b,
    send_a2,
    recv_a2,
    send_b2,
    recv_b2,
    track_a1,
    track_b1,
    trk_a,
    trk_raw,
    trk_b,
    mid_out,
    mid_in,
    grad_a1,
    grad_b1,
    grad_a,
    grad_b,
    loss_out,
    loss_in,
    hg,
    hg_sum,
    ga_mine,
    ga_send,
    ga_recv,
    dots,
    dots_in,
    load_sem,
    send_sem,
    recv_sem,
):
    ny, nz, nx = dims
    nseq = ny * nz * nx
    planes = ny * nx
    rows, half = out_v.shape
    padded = rows + 2 * STEP
    width = 2 * half
    gl = track.shape[0]
    genes = gl * nseq
    group_a = gl * nz
    group_b = gl * planes
    each = gl // CHUNKS
    part_a = each * nz
    part_b = each * planes
    part = each * nseq
    cols = half // 3
    wide_a = 2 * cols
    first_sem, _ = phases()
    me = lax.axis_index("seq")
    c = lax.axis_index("chan")
    oc = 1 - c
    x = lax.rem(me, nx)
    z = lax.rem(lax.div(me, nx), nz)
    y = lax.div(me, nx * nz)
    p = y * nx + x
    nxt = lax.rem(me + 1, nseq)
    prv = lax.rem(me + nseq - 1, nseq)

    def plane_at(q):
        return (lax.div(q, nx) * nz + z) * nx + lax.rem(q, nx)

    def plane_to(k):
        return lax.rem(p + k, planes)

    def plane_from(k):
        return lax.rem(p + planes - k, planes)

    def z_at(q):
        return (y * nz + q) * nx + x

    def z_to(k):
        return lax.rem(z + k, nz)

    def z_from(k):
        return lax.rem(z + nz - k, nz)

    plane_q = [plane_to(k) for k in range(planes)]
    plane_id = [plane_at(q) for q in plane_q]
    z_q = [z_to(k) for k in range(nz)]
    z_id = [z_at(q) for q in z_q]

    def rows_a(q):
        return pl.ds(pl.multiple_of(q * group_a, group_a), group_a)

    def rows_b(q):
        return pl.ds(pl.multiple_of(q * group_b, group_b), group_b)

    def chunk_a(n, q):
        return pl.ds(pl.multiple_of(n * part + q * part_a, part_a), part_a)

    def chunk_b(n, q):
        return pl.ds(pl.multiple_of(n * part + q * part_b, part_b), part_b)

    def chunk_rows(n):
        return slice(n * part, (n + 1) * part)

    def loop(lo, hi, body, unroll=1):
        def step(i, carry):
            body(i)
            return carry

        lax.fori_loop(lo, hi, step, 0, unroll=unroll)

    def remote(src, dst, name, k, seq, chan):
        return pltpu.make_async_remote_copy(
            src_ref=src,
            dst_ref=dst,
            send_sem=send_sem.at[first_sem[name] + k],
            recv_sem=recv_sem.at[first_sem[name] + k],
            device_id=(seq, chan),
            device_id_type=MESH,
        )

    barrier = pltpu.get_barrier_semaphore()

    def greet(seq, chan):
        pl.semaphore_signal(barrier, inc=1, device_id=(seq, chan), device_id_type=MESH)

    for k in range(1, nz):
        greet(z_id[k], c)
    for k in range(1, planes):
        greet(plane_id[k], c)
    greet(nxt, c)
    greet(prv, c)
    greet(me, oc)

    def all_in(of, name, k=0):
        pltpu.make_async_copy(of, of, recv_sem.at[first_sem[name] + k]).wait()

    def all_out(of, name, k=0):
        pltpu.make_async_copy(of, of, send_sem.at[first_sem[name] + k]).wait()

    others_z = pl.ds(0, nz - 1)
    others_p = pl.ds(0, planes - 1)

    mid_rows = pl.ds(STEP, rows)
    smalls = [
        pltpu.make_async_copy(src, dst, load_sem.at[4 + i])
        for i, (src, dst) in enumerate(
            (
                (track_hbm, track),
                (start_hbm, start),
                (end_hbm, end),
                (owner_hbm, owner),
                (gain_hbm, gain),
                (positive_hbm, positive),
            )
        )
    ]
    load_x = pltpu.make_async_copy(x_hbm, xp.at[c, mid_rows], load_sem.at[0])
    load_w = [
        pltpu.make_async_copy(w_hbm.at[k], w.at[k], load_sem.at[1 + k]) for k in range(TAPS)
    ]
    for copy in smalls:
        copy.start()
    load_x.start()
    pl.semaphore_wait(barrier, 3 + planes - 1 + nz - 1)

    piece = STEP // PIECES

    def to_next(i):
        src = pl.ds(rows - STEP + i * piece, piece)
        return remote(x_hbm.at[src], xp.at[c, pl.ds(i * piece, piece)], "next", i, nxt, c)

    def to_prev(i):
        src = pl.ds(i * piece, piece)
        dst = pl.ds(STEP + rows + i * piece, piece)
        return remote(x_hbm.at[src], xp.at[c, dst], "prev", i, prv, c)

    def core(side):
        return remote(x_hbm, xp.at[side, mid_rows], "core", 0, me, oc)

    def left(side, i):
        some = pl.ds(i * piece, piece)
        return remote(xp.at[side, some], xp.at[side, some], "left", i, me, oc)

    def right(side, i):
        some = pl.ds(STEP + rows + i * piece, piece)
        return remote(xp.at[side, some], xp.at[side, some], "right", i, me, oc)

    core(c).start()
    to_next(0).start()
    to_prev(0).start()

    def gather_a1(buf, name, k, slot):
        return remote(buf.at[z], buf.at[slot], name, 0, z_id[k], c)

    def gather_b1(buf, name, k, slot):
        return remote(buf.at[p], buf.at[slot], name, 0, plane_id[k], c)

    def gather_a2(buf, name, k, q):
        return remote(buf.at[rows_a(p)], buf.at[rows_a(q)], name, 0, plane_id[k], c)

    def gather_b2(buf, name, k, q):
        return remote(buf.at[rows_b(z)], buf.at[rows_b(q)], name, 0, z_id[k], c)

    for copy in smalls:
        copy.wait()
    own_track = track[...].astype(F32)
    track_b1[p] = own_track[:, wide_a:half]
    for k in range(1, planes):
        gather_b1(track_b1, "track_b1", k, p).start()
    track_a1[z] = own_track[:, 0:wide_a]
    for k in range(1, nz):
        gather_a1(track_a1, "track_a1", k, z).start()
    to_next(1).start()
    to_prev(1).start()
    for copy in load_w:
        copy.start()

    first = start[...]
    last = end[...]
    slot_of = chunk_order(owner[...], dims, gl)
    spans = first.shape[1]
    base = me * rows - STEP

    def member_rows(i):
        at = pl.multiple_of(i * ROWS, ROWS)
        bins = base + at + lax.broadcasted_iota(jnp.int32, (ROWS, spans), 0)
        inside = (first <= bins) & (bins < last)
        member[pl.ds(at, ROWS), :] = jnp.where(inside, 1.0, 0.0).astype(BF16)

    def owner_rows(i):
        at = pl.multiple_of(i * ROWS, ROWS)
        gene = at + lax.broadcasted_iota(jnp.int32, (ROWS, spans), 0)
        own_hot[pl.ds(at, ROWS), :] = jnp.where(slot_of == gene, 1.0, 0.0).astype(BF16)

    def perm_rows(i):
        at = pl.multiple_of(i * ROWS, ROWS)
        down = at + lax.broadcasted_iota(jnp.int32, (ROWS, genes), 0)
        across = lax.broadcasted_iota(jnp.int32, (1, genes), 1)
        row = at + lax.broadcasted_iota(jnp.int32, (ROWS, 1), 0)
        some = pl.ds(at, ROWS)
        moved = second_from_first(row, dims, gl)
        perm_k[some, :] = jnp.where(across == moved, 1.0, 0.0).astype(BF16)
        moved = second_from_chunk(row, dims, gl)
        perm[some, :] = jnp.where(across == moved, 1.0, 0.0).astype(BF16)
        across = second_from_chunk(across, dims, gl)
        perm_t[some, :] = jnp.where(across == down, 1.0, 0.0).astype(BF16)

    loop(0, genes // ROWS, owner_rows)
    loop(0, padded // ROWS, member_rows)

    def normed_rows(at):
        some = pl.ds(at, ROWS)
        x0 = xp[0, some, :].astype(F32)
        x1 = xp[1, some, :].astype(F32)
        total = jnp.sum(x0 * x0, axis=1, keepdims=True) + jnp.sum(x1 * x1, axis=1, keepdims=True)
        root = lax.rsqrt(total / width + EPS)
        return (x0, x1), root

    def gain_of(h):
        return gain[h * half : (h + 1) * half].reshape(1, half)

    def gelu(n):
        return 0.5 * n * (1.0 + jnp.tanh(GELU_A * (n + GELU_B * n * n * n)))

    def gelu_slope(n):
        t = jnp.tanh(GELU_A * (n + GELU_B * n * n * n))
        return 0.5 * (1.0 + t) + 0.5 * n * (1.0 - t * t) * (
            GELU_A * (1.0 + 3.0 * GELU_B * n * n)
        )

    def activate(lo, count, keep):
        def body(i):
            at = pl.multiple_of(lo + i * ROWS, ROWS)
            xs, root = normed_rows(at)
            for h in range(2):
                act[h, pl.ds(at, ROWS), :] = (gelu(xs[h] * root * gain_of(h)) * keep).astype(BF16)

        loop(0, count // ROWS, body)

    load_x.wait()
    core(oc).wait_recv()
    activate(STEP, rows, 1.0)

    for copy in load_w:
        copy.wait()

    def tap(lo, count, k, some):
        return dot_nn(act[0, lo : lo + count, :], w[k, 0:half, some]) + dot_nn(
            act[1, lo : lo + count, :], w[k, half:width, some]
        )

    def centre_cols(i):
        some = pl.ds(pl.multiple_of(i * cols, cols), cols)
        acc[:, some] = xp[c, mid_rows, some].astype(F32) + tap(STEP, rows, 1, some)
        acc[0:STEP, some] += tap(rows, STEP, 2, some)
        acc[STEP:rows, some] += tap(STEP, STEP, 0, some)

    loop(0, half // cols, centre_cols)

    def gather_turn(a1, b1, a2, b2, name):
        all_in(a1.at[others_z], name + "_a1")
        for i in range(nz):
            tmp_a[i * gl : (i + 1) * gl, :] = a1[i, :, 0:wide_a]
        a2[rows_a(p), :] = tmp_a[...].astype(BF16)
        for k in range(1, planes):
            gather_a2(a2, name + "_a2", k, p).start()

        all_in(b1.at[others_p], name + "_b1")
        for i in range(planes):
            tmp_b[i * gl : (i + 1) * gl, :] = b1[i]
        b2[rows_b(z), :] = tmp_b[...].astype(BF16)
        for k in range(1, nz):
            gather_b2(b2, name + "_b2", k, z).start()

    def gather_end_a(a2, name):
        all_in(a2.at[pl.ds(0, (planes - 1) * group_a)], name + "_a2")

    def gather_end_b(b2, name):
        all_in(b2.at[pl.ds(0, (nz - 1) * group_b)], name + "_b2")

    gather_turn(track_a1, track_b1, trk_a, trk_raw, "track")

    keep_left = jnp.where(me > 0, 1.0, 0.0)
    keep_right = jnp.where(me < nseq - 1, 1.0, 0.0)
    for i in range(PIECES):
        to_next(i).wait_recv()
        left(c, i).start()
        to_prev(i).wait_recv()
        right(c, i).start()
        if i == 0:
            counts[...] = dot_nt(own_hot[...], member[mid_rows, :]).astype(BF16)
            loop(0, genes // ROWS, perm_rows)
        else:
            counts_b[...] = dot_nn(perm_t[...], counts[...]).astype(BF16)
        left(oc, i).wait_recv()
        activate(i * piece, piece, keep_left)
        right(oc, i).wait_recv()
        activate(STEP + rows + i * piece, piece, keep_right)

    def hidden_cols(i):
        some = slice(i * cols, (i + 1) * cols)
        hid[0:STEP, some] = (acc[0:STEP, some] + tap(0, STEP, 0, some)).astype(BF16)
        hid[STEP:rows, some] = (acc[STEP:rows, some] + tap(STEP + rows, STEP, 2, some)).astype(BF16)

    def pool_b1(n, k):
        q = z_q[k]
        return remote(send_b.at[chunk_b(n, q)], recv_b.at[n, k], "pool_b1", n, z_id[k], c)

    def pool_a1(n, k):
        q = plane_q[k]
        return remote(
            send_a.at[chunk_a(n, q)], recv_a.at[n, k], "pool_a1", n, plane_id[k], c
        )

    for n in range(CHUNKS):
        some = chunk_rows(n)
        for i in range(2):
            tile = slice(i * cols, (i + 1) * cols)
            if n == 0:
                hidden_cols(i)
            send_a[some, tile] = dot_nn(counts[some, :], hid[:, tile]).astype(BF16)
        for k in range(1, planes):
            pool_a1(n, k).start()
        if n == 0:
            hidden_cols(2)
        send_b[some, :] = dot_nn(counts_b[some, :], hid[:, wide_a:half]).astype(BF16)
        for k in range(1, nz):
            pool_b1(n, k).start()

    def factor_rows(i):
        at = pl.multiple_of(i * ROWS, ROWS)
        some = pl.ds(at, ROWS)
        xs, root = normed_rows(STEP + at)
        mine = jnp.where(c == 0, xs[0], xs[1])
        g = jnp.where(c == 0, gain_of(0), gain_of(1))
        fac[some, :] = gelu_slope(mine * root * g) * (root * g)
        xq[some, :] = mine * (root * root / width)

    tile = min(256, genes)
    for i in range(genes // tile):
        some = slice(i * tile, (i + 1) * tile)
        counts_t[:, some] = dot_nt(member[...], own_hot[some, :]).astype(BF16)
    for i in range(genes // tile):
        some = slice(i * tile, (i + 1) * tile)
        counts_tb[:, some] = dot_nn(counts_t[...], perm[:, some]).astype(BF16)

    def pool_b2(n, k):
        q = plane_q[k]
        return remote(
            send_b2.at[n, q], recv_b2.at[n, k], "pool_b2", n, plane_id[k], c
        )

    def pool_a2(n, k):
        q = z_q[k]
        return remote(send_a2.at[n, q], recv_a2.at[n, k], "pool_a2", n, z_id[k], c)

    for n in range(CHUNKS):

        part_sum = send_a[chunk_a(n, p), :].astype(F32)
        all_in(recv_a.at[n, others_p], "pool_a1", n)
        for k in range(1, planes):
            part_sum = part_sum + recv_a[n, k].astype(F32)
        for i in range(nz):
            send_a2[n, i] = part_sum[i * each : (i + 1) * each, :]
        for k in range(1, nz):
            pool_a2(n, k).start()

        part_sum = send_b[chunk_b(n, z), :].astype(F32)
        all_in(recv_b.at[n, others_z], "pool_b1", n)
        for k in range(1, nz):
            part_sum = part_sum + recv_b[n, k].astype(F32)
        for i in range(planes):
            send_b2[n, i] = part_sum[i * each : (i + 1) * each, :]
        for k in range(1, planes):
            pool_b2(n, k).start()

    gather_end_a(trk_a, "track")
    gather_end_b(trk_raw, "track")
    trk_b[...] = dot_nn(perm_k[...], trk_raw[...]).astype(BF16)

    def grad_a1_copy(n, k, slot):
        return remote(
            grad_a1.at[n, z], grad_a1.at[n, slot], "grad_a1", n, z_id[k], c
        )

    def grad_b1_copy(n, k, slot):
        return remote(
            grad_b1.at[n, p],
            grad_b1.at[n, slot],
            "grad_b1",
            n,
            plane_id[k],
            c,
        )

    def grad_a2_copy(n, k, q):
        return remote(
            grad_a.at[chunk_a(n, p)],
            grad_a.at[chunk_a(n, q)],
            "grad_a2",
            n,
            plane_id[k],
            c,
        )

    def grad_b2_copy(n, k, q):
        return remote(
            grad_b.at[chunk_b(n, z)],
            grad_b.at[chunk_b(n, q)],
            "grad_b2",
            n,
            z_id[k],
            c,
        )

    def mid_copy(n):
        return remote(mid_out.at[n], mid_in.at[n], "mid", n, me, oc)

    for n in range(CHUNKS):

        mine_b = send_b2[n, p]
        all_in(recv_b2.at[n, others_p], "pool_b2", n)
        for k in range(1, planes):
            mine_b = mine_b + recv_b2[n, k]
        mine_a = send_a2[n, z]
        all_in(recv_a2.at[n, others_z], "pool_a2", n)
        for k in range(1, nz):
            mine_a = mine_a + recv_a2[n, k]
        raw_part = dot_nt(mine_a.astype(BF16), trk_a[...]) + dot_nt(
            mine_b.astype(BF16), trk_b[...]
        )
        sq_part = jnp.sum(mine_a * mine_a, axis=1, keepdims=True) + jnp.sum(
            mine_b * mine_b, axis=1, keepdims=True
        )
        mid_out[n, :, 0:genes] = raw_part
        mid_out[n, :, genes : genes + 128] = jnp.broadcast_to(sq_part, (each, 128))
        mid_copy(n).start()
        mid_copy(n).wait_recv()
        both = mid_out[n] + mid_in[n]
        raw = both[:, 0:genes]
        scale = lax.rsqrt(both[:, genes : genes + 1] / width + EPS)
        unit = float(width) ** -0.5
        logits = raw * (scale * (INV_TEMP * unit))
        top = jnp.max(logits, axis=1, keepdims=True)
        log_total = top + jnp.log(jnp.sum(jnp.exp(logits - top), axis=1, keepdims=True))
        place = lax.broadcasted_iota(jnp.int32, (each, genes), 0)
        want = jnp.zeros((each, genes), jnp.int32)
        for i in range(each):
            want = jnp.where(place == i, first_order(positive[n * each + i], dims, gl), want)
        hits = lax.broadcasted_iota(jnp.int32, (each, genes), 1) == want
        weights = jnp.exp(logits - log_total)
        grad_logit = (LOSS_SCALE * (weights - jnp.where(hits, 1.0, 0.0))).astype(BF16)
        inner = INV_TEMP * jnp.sum(grad_logit.astype(F32) * raw, axis=1, keepdims=True)
        back = inner * scale * scale / width
        outer = unit * scale
        per_gene = log_total - jnp.sum(jnp.where(hits, logits, 0.0), axis=1, keepdims=True)
        grad_a1[n, z, :, 0:wide_a] = outer * (
            INV_TEMP * dot_nn(grad_logit, trk_a[...]) - mine_a * back
        )
        grad_a1[n, z, :, wide_a : wide_a + 128] = jnp.broadcast_to(per_gene, (each, 128))
        for k in range(1, nz):
            grad_a1_copy(n, k, z).start()
        grad_b1[n, p] = outer * (INV_TEMP * dot_nn(grad_logit, trk_b[...]) - mine_b * back)
        for k in range(1, planes):
            grad_b1_copy(n, k, p).start()

    for n in range(CHUNKS):

        all_in(grad_b1.at[n, others_p], "grad_b1", n)
        for i in range(planes):
            tmp_b[i * each : (i + 1) * each, :] = grad_b1[n, i]
        grad_b[chunk_b(n, z), :] = tmp_b[0:part_b, :].astype(BF16)
        for k in range(1, nz):
            grad_b2_copy(n, k, z).start()

        all_in(grad_a1.at[n, others_z], "grad_a1", n)
        for i in range(nz):
            tmp_a[i * each : (i + 1) * each, :] = grad_a1[n, i, :, 0:wide_a]
        grad_a[chunk_a(n, p), :] = tmp_a[0:part_a, :].astype(BF16)
        for k in range(1, planes):
            grad_a2_copy(n, k, p).start()

    some_loss = jnp.zeros((1, 128), F32)
    for n in range(CHUNKS):
        for i in range(nz):
            some_loss = some_loss + jnp.sum(
                grad_a1[n, i, :, wide_a : wide_a + 128], axis=0, keepdims=True
            )
    loss_out[...] = jnp.broadcast_to(some_loss, (8, 128))
    loss_in[p] = loss_out[...]

    def loss_copy(k, q):
        return remote(loss_out, loss_in.at[q], "loss", 0, plane_id[k], c)

    for k in range(1, planes):
        loss_copy(k, p).start()

    loop(0, rows // ROWS, factor_rows)

    for n in range(CHUNKS):
        some = chunk_rows(n)

        all_in(grad_b.at[pl.ds(0, (nz - 1) * part_b)], "grad_b2", n)
        for i in (2, 0, 1):
            tile = slice(i * cols, (i + 1) * cols)
            if i == 2:
                total = dot_nn(counts_tb[:, some], grad_b[some, :])
            else:
                if i == 0:
                    all_in(grad_a.at[pl.ds(0, (planes - 1) * part_a)], "grad_a2", n)
                total = dot_nn(counts_t[:, some], grad_a[some, tile])
            if n > 0:
                total = total + hg_sum[:, tile]
            if n < CHUNKS - 1:
                hg_sum[:, tile] = total
            else:
                hg[:, tile] = total.astype(BF16)

    def activ_grad(h, i):
        wide = pl.ds(pl.multiple_of(h * half + i * cols, cols), cols)
        total = jnp.zeros((rows, cols), F32)
        for k in range(TAPS):
            lo = (TAPS - 1 - k) * STEP
            total = total + dot_nt(hg[lo : lo + rows, :], w[k, wide, :])
        return total

    def grad_copy(i):
        return remote(ga_send.at[i], ga_recv.at[i], "last", i, me, oc)

    for i in range(3):
        ga_send[i] = activ_grad(oc, i).astype(BF16)
        grad_copy(i).start()
    for i in range(3):
        ga_mine[:, i * cols : (i + 1) * cols] = activ_grad(c, i)

    for i in range(3):
        grad_copy(i).wait_recv()
    part_rows = rows // PIECES

    def dots_copy(i):
        return remote(dots.at[i], dots_in.at[i], "dots", i, me, oc)

    for i in range(PIECES):

        def weigh(j):
            at = pl.multiple_of(j * ROWS, ROWS)
            some = pl.ds(i * part_rows + at, ROWS)
            wide = pl.ds(STEP + i * part_rows + at, ROWS)
            got = jnp.concatenate([ga_recv[n, some, :] for n in range(3)], axis=1)
            v = fac[some, :] * (ga_mine[some, :] + got.astype(F32))
            out_v[some, :] = v
            inner = jnp.sum(xp[c, wide, :].astype(F32) * v, axis=1, keepdims=True)
            dots[i, pl.ds(at, ROWS), :] = jnp.broadcast_to(inner, (ROWS, 128))

        loop(0, part_rows // ROWS, weigh, unroll=True)
        dots_copy(i).start()
    all_in(loss_in.at[others_p], "loss")
    total_loss = jnp.zeros((8, 128), F32)
    for i in range(planes):
        total_loss = total_loss + loss_in[i]
    loss_ref[...] = total_loss / genes
    for i in range(PIECES):
        dots_copy(i).wait_recv()

        def finish(j):
            at = pl.multiple_of(j * ROWS, ROWS)
            some = pl.ds(i * part_rows + at, ROWS)
            wide = pl.ds(STEP + i * part_rows + at, ROWS)
            inner = (dots[i, pl.ds(at, ROWS), :] + dots_in[i, pl.ds(at, ROWS), :])[:, 0:1]
            out_v[some, :] = out_v[some, :] + (hg[wide, :].astype(F32) - xq[some, :] * inner)

        loop(0, part_rows // ROWS, finish, unroll=True)
    for i in range(PIECES):
        to_next(i).wait_send()
        to_prev(i).wait_send()
        left(c, i).wait_send()
        right(c, i).wait_send()
    core(c).wait_send()

    all_out(track_a1.at[others_z], "track_a1")
    all_out(track_b1.at[others_p], "track_b1")
    all_out(trk_a.at[pl.ds(0, (planes - 1) * group_a)], "track_a2")
    all_out(trk_raw.at[pl.ds(0, (nz - 1) * group_b)], "track_b2")
    all_out(loss_in.at[others_p], "loss")
    for n in range(CHUNKS):
        all_out(recv_a.at[n, others_p], "pool_a1", n)
        all_out(recv_b.at[n, others_z], "pool_b1", n)
        all_out(recv_a2.at[n, others_z], "pool_a2", n)
        all_out(recv_b2.at[n, others_p], "pool_b2", n)
        all_out(grad_a1.at[n, others_z], "grad_a1", n)
        all_out(grad_b1.at[n, others_p], "grad_b1", n)
        all_out(grad_a.at[pl.ds(0, (planes - 1) * part_a)], "grad_a2", n)
        all_out(grad_b.at[pl.ds(0, (nz - 1) * part_b)], "grad_b2", n)
    for n in range(CHUNKS):
        mid_copy(n).wait_send()
    for i in range(3):
        grad_copy(i).wait_send()
    for i in range(PIECES):
        dots_copy(i).wait_send()


def per_device(dims, stop, x, weight, gain, track, start, end, owner, positive):
    ny, nz, nx = dims
    nseq, planes = ny * nz * nx, ny * nx
    rows, half = x.shape
    gl = track.shape[0]
    genes, spans = gl * nseq, start.shape[0]
    group_a, group_b = gl * nz, gl * planes
    padded = rows + 2 * STEP
    each = gl // CHUNKS
    cols = half // 3
    wide_a = 2 * cols
    copies = phases()[1]
    dma = pltpu.SemaphoreType.DMA
    vmem = pl.BlockSpec(memory_space=pltpu.VMEM)
    scratch = [
        pltpu.VMEM((2 * half,), F32),
        pltpu.VMEM((gl, half), BF16),
        pltpu.VMEM((1, spans), jnp.int32),
        pltpu.VMEM((1, spans), jnp.int32),
        pltpu.VMEM((1, spans), jnp.int32),
        pltpu.SMEM((gl,), jnp.int32),
        pltpu.VMEM((2, padded, half), BF16),
        pltpu.VMEM((TAPS, 2 * half, half), BF16),
        pltpu.VMEM((2, padded, half), BF16),
        pltpu.VMEM((rows, half), F32),
        pltpu.VMEM((rows, half), F32),
        pltpu.VMEM((genes, spans), BF16),
        pltpu.VMEM((padded, spans), BF16),
        pltpu.VMEM((genes, rows), BF16),
        pltpu.VMEM((padded, genes), BF16),
        pltpu.VMEM((genes, rows), BF16),
        pltpu.VMEM((padded, genes), BF16),
        pltpu.VMEM((genes, genes), BF16),
        pltpu.VMEM((genes, genes), BF16),
        pltpu.VMEM((genes, genes), BF16),
        pltpu.VMEM((rows, half), F32),
        pltpu.VMEM((rows, half), BF16),
        pltpu.VMEM((genes, wide_a), BF16),
        pltpu.VMEM((CHUNKS, planes, each * nz, wide_a), BF16),
        pltpu.VMEM((genes, cols), BF16),
        pltpu.VMEM((CHUNKS, nz, each * planes, cols), BF16),
        pltpu.VMEM((group_a, wide_a), F32),
        pltpu.VMEM((group_b, cols), F32),
        pltpu.VMEM((CHUNKS, nz, each, wide_a), F32),
        pltpu.VMEM((CHUNKS, nz, each, wide_a), F32),
        pltpu.VMEM((CHUNKS, planes, each, cols), F32),
        pltpu.VMEM((CHUNKS, planes, each, cols), F32),
        pltpu.VMEM((nz, gl, wide_a), F32),
        pltpu.VMEM((planes, gl, cols), F32),
        pltpu.VMEM((genes, wide_a), BF16),
        pltpu.VMEM((genes, cols), BF16),
        pltpu.VMEM((genes, cols), BF16),
        pltpu.VMEM((CHUNKS, each, genes + 128), F32),
        pltpu.VMEM((CHUNKS, each, genes + 128), F32),
        pltpu.VMEM((CHUNKS, nz, each, wide_a + 128), F32),
        pltpu.VMEM((CHUNKS, planes, each, cols), F32),
        pltpu.VMEM((genes, wide_a), BF16),
        pltpu.VMEM((genes, cols), BF16),
        pltpu.VMEM((8, 128), F32),
        pltpu.VMEM((planes, 8, 128), F32),
        pltpu.VMEM((padded, half), BF16),
        pltpu.VMEM((padded, half), F32),
        pltpu.VMEM((rows, half), F32),
        pltpu.VMEM((3, rows, cols), BF16),
        pltpu.VMEM((3, rows, cols), BF16),
        pltpu.VMEM((PIECES, rows // PIECES, 128), F32),
        pltpu.VMEM((PIECES, rows // PIECES, 128), F32),
        dma((10,)),
        dma((copies,)),
        dma((copies,)),
    ]
    grad, loss = pl.pallas_call(
        functools.partial(kernel, dims, stop),
        out_shape=(
            jax.ShapeDtypeStruct((rows, half), F32),
            jax.ShapeDtypeStruct((8, 128), F32),
        ),
        in_specs=[pl.BlockSpec(memory_space=pltpu.HBM)] * 8,
        out_specs=(vmem, vmem),
        scratch_shapes=scratch,
        compiler_params=pltpu.CompilerParams(
            collective_id=0, has_side_effects=True, vmem_limit_bytes=48 * 1024 * 1024
        ),
    )(
        *(
            pltpu.with_memory_space_constraint(array, pltpu.HBM)
            for array in (
                x,
                weight,
                gain,
                track,
                start.reshape(1, -1),
                end.reshape(1, -1),
                owner.reshape(1, -1),
                positive,
            )
        )
    )
    return grad, loss[0, 0]


def solution(mesh, dims=(4, 8, 4), stop=99):
    return jax.shard_map(
        functools.partial(per_device, dims, stop),
        mesh=mesh,
        in_specs=(
            P("seq", "chan"),
            P(None, None, "chan"),
            P(),
            P("seq", "chan"),
            P(),
            P(),
            P(),
            P("seq"),
        ),
        out_specs=(P("seq", "chan"), P()),
        check_vma=False,
    )
```
